32 devices in a mesh: batch: 4 (over y, x), seq: 8 (over z, core).
Axes of the slice: x: 2, y: 2, z: 4, core: 2. Of those that a mesh axis runs over, the one named last changes fastest.
Arguments:
- queries: bfloat16 [4, 2048, 1024], P('batch', 'seq'), may hold values from -6 to 6
- key_states: bfloat16 [4, 2048, 1024], P('batch', 'seq'), may hold values from -6 to 6
- value_states: bfloat16 [4, 2048, 1024], P('batch', 'seq'), may hold values from -6 to 6
- out_grad: bfloat16 [4, 2048, 1024], P('batch', 'seq'), may hold values from -6 to 6
- memory: float32 [1024, 1024], replicated, may hold values from -6 to 6
- near_device: int32 [16, 4], replicated, may hold values from 0 to 7, all different within a row; in each aligned block of 2 rows (0 to 1, 2 to 3, ...) no two rows name the same one
- near_slot: int32 [16, 4], replicated, may hold values from 0 to 1
- near_count: int32 [16], replicated, may hold values from 1 to 4, 40 in all
- writer_block: int32 [1024], replicated, may hold values from 0 to 15, as said below
Outputs:
- attended: bfloat16 [4, 2048, 1024], P('batch', 'seq')
- query_grad: bfloat16 [4, 2048, 1024], P('batch', 'seq')
- key_grad: bfloat16 [4, 2048, 1024], P('batch', 'seq')
- value_grad: bfloat16 [4, 2048, 1024], P('batch', 'seq')
- memory_grad: float32 [1024, 1024], P('seq')
The draws below stay inside these ranges and needn't reach their ends.
Inputs may be any that keep to these rules, and one draw needn't show every extreme that they name: Row n of near_device belongs to block n; one row names different indices; the rows of the 2 blocks of one index of seq name no index more than 1 times. writer_block[r] // 2 == r // 128: a memory row is written by a block of the index of seq that holds the row.
All inputs are finite; a program needn't handle non-finite values.
Results may differ from the reference program's by a relative error of at most 0.025.
Values may be sent and summed in bfloat16 or wider, within the bound.
A program may use at most 192 MiB of HBM per device.

```python
import math
import jax
import jax.numpy as jnp
import numpy as np
from jax import lax

HEADS = 8
HD = 128
BLK = 128
NEAR = 4
MEM = 1024
HW = 1024
BLK_DEV = 2
SEQ = 2048
BLOCKS = 16
BATCH = 4
ROWS_DEV = 128
CAP = 1
N_SEQ = 8


def draw_queries(key, part):
    base_key = jax.random.fold_in(key, 11)
    return jnp.clip(jax.random.normal(base_key, (BATCH, SEQ, HW), jnp.float32), -6.0, 6.0).astype(jnp.bfloat16)


def draw_memory(key, part):
    base_key = jax.random.fold_in(key, 23)
    return jnp.clip(jax.random.normal(base_key, (MEM, HW), jnp.float32), -6.0, 6.0)


def draw_writer_block(key, part):
    row_index = jnp.arange(MEM, dtype=jnp.int32)
    within = row_index % ROWS_DEV
    chosen_slot = jax.random.randint(jax.random.fold_in(key, 37), (MEM,), 0, BLK_DEV, dtype=jnp.int32)
    chosen_slot = jnp.where(within == 0, 0, jnp.where(within == ROWS_DEV - 1, BLK_DEV - 1, chosen_slot))
    return (row_index // ROWS_DEV * BLK_DEV + chosen_slot).astype(jnp.int32)


def plant(values, rng, low, largest):
    index_at = [jax.random.randint(jax.random.fold_in(rng, axis), (), 0, length) for axis, length in enumerate(values.shape)]
    main_axis = values.shape.index(max(values.shape))
    neighbour = index_at[:main_axis] + [(index_at[main_axis] + 1) % values.shape[main_axis]] + index_at[main_axis + 1:]
    return values.at[tuple(index_at)].set(low).at[tuple(neighbour)].set(largest)


def steps_of(key, dims, split, low, high):
    def one(axis_at, shards_of):
        steps = jax.random.uniform(jax.random.fold_in(jax.random.fold_in(key, 6), axis_at), (shards_of,), jnp.float32, low / len(split), high / len(split))
        return jnp.repeat(jnp.exp(steps), dims[axis_at] // shards_of).reshape((-1,) + (1,) * (len(dims) - axis_at - 1))

    gain = one(*split[0])
    for cut in split[1:]:
        gain = gain * one(*cut)
    return gain


def length_profile(count, total, most, slope):
    loads = [(1 << 20) // math.isqrt(standing ** slope) + 1 for standing in range(2, count + 1)]
    surplus, holding = total - most - (count - 1), [1] * (count - 1)
    while surplus > 0:
        candidates = [i for i in range(count - 1) if holding[i] < most]
        pool, budget = sum([loads[i] for i in candidates]), surplus
        for i in candidates:
            more = min(most - holding[i], max(1, budget * loads[i] // pool), surplus)
            holding[i] = holding[i] + more
            surplus = surplus - more
    return np.array([most] + holding)


def uneven_parts(rng, amount, total, bound, lean):
    if amount == 2:
        one = jax.random.randint(rng, (), max(1, total - bound), min(bound, total - 1) + 1)
        return jnp.stack([one, total - one])
    sizes = jnp.asarray(length_profile(amount, total, bound, lean), jnp.int32)
    couples = (amount - 1) // 2
    source_of, sink = sizes[1:1 + 2 * couples:2], sizes[2:2 + 2 * couples:2]
    room = jnp.minimum(source_of - 1, bound - sink)
    shifted = jax.random.randint(jax.random.fold_in(rng, 1), (couples,), 0, 1 << 20) % (room + 1)
    sizes = sizes.at[1:1 + 2 * couples:2].set(source_of - shifted).at[2:2 + 2 * couples:2].set(sink + shifted)
    return sizes[jax.random.permutation(jax.random.fold_in(rng, 2), amount)]


def shared_out(stream_key, own, number, rows, number_of, top, bound, slope):
    ranking = jax.random.permutation(stream_key, number_of)
    packed, ordinary = load_shares(number_of, rows * top, bound, slope, True), load_shares(number_of, rows * top, bound, slope, False)
    places = jnp.arange(number_of)

    def named(sizes, offset_by):
        used = int((sizes > 0).sum())
        fixed = max(1, used // 4)
        moved = fixed + (places - fixed + offset_by * (used - fixed)) % max(1, number_of - fixed)
        return jnp.zeros((number_of,), jnp.int32).at[ranking[jnp.where(places < fixed, places, moved)]].set(jnp.asarray(sizes, jnp.int32))

    sizes = jnp.where(number % 4 == 0, named(packed, number // 4), named(ordinary, number - number // 4 - 1))
    mixed = jax.random.permutation(jax.random.fold_in(own, 3), number_of)
    giver, taker = mixed[0:number_of // 2 * 2:2], mixed[1:number_of // 2 * 2:2]
    margin = jnp.minimum(sizes[giver] - 1, bound - sizes[taker]) // 2
    margin = jnp.where((giver == ranking[0]) | (taker == ranking[0]) | (sizes[taker] == 0), 0, jnp.maximum(margin, 0))
    moved = jax.random.randint(jax.random.fold_in(own, 4), (number_of // 2,), 0, 1 << 20) % (margin + 1)
    sizes = sizes.at[giver].add(-moved).at[taker].add(moved)
    items = jnp.searchsorted(jnp.cumsum(sizes), jnp.arange(rows * top), side="right").astype(jnp.int32)
    table = items.reshape(top, rows).T
    table = table[jax.random.permutation(jax.random.fold_in(own, 1), rows)]
    offset_by = jax.random.randint(jax.random.fold_in(own, 2), (rows, 1), 0, top)
    return jnp.take_along_axis(table, (jnp.arange(top)[None, :] + offset_by) % top, axis=1)


def load_shares(number_of, total, reach, lean, full):
    weights = [(1 << 20) // math.isqrt(grade ** lean) + 1 for grade in range(1, number_of + 1)]
    largest = reach if full else min(reach, max(-(-total // number_of), total * weights[0] // sum(weights)))
    least = 1 if total - largest >= number_of - 1 else 0
    holding, surplus = [largest] + [least] * (number_of - 1), total - largest - least * (number_of - 1)
    while surplus > 0:
        movable = [i for i in range(1, number_of) if holding[i] < largest] or [i for i in range(1, number_of) if holding[i] < reach]
        whole, left = sum([weights[i] for i in movable]), surplus
        for i in movable:
            extra = min(reach - holding[i], max(1, left * weights[i] // whole), surplus)
            holding[i] = holding[i] + extra
            surplus = surplus - extra
    return np.array(holding)


def gaussian(key, shape, width, reach, shards=(), held_as=jnp.bfloat16):
    values = jax.random.normal(key, shape, jnp.float32) * width
    if len(shards) > 0:
        values = steps_of(key, shape, shards, -0.22, 0.18) * values
    return jnp.clip(values, min=-reach, max=reach).astype(held_as)


def setup_inputs(seed: int = 0) -> dict:
    arg_keys = jax.random.split(jax.random.key(seed), 10)
    queries = draw_queries(jax.random.fold_in(arg_keys[9], 71), 0)
    key_states = gaussian(arg_keys[1], (BATCH, SEQ, HW), 1.0, 6.0, ((0, 4), (1, 8)))
    value_states = gaussian(arg_keys[2], (BATCH, SEQ, HW), 1.0, 6.0, ((0, 4), (1, 8)))
    out_grad = gaussian(arg_keys[3], (BATCH, SEQ, HW), 1.0, 6.0, ((0, 4), (1, 8)))
    memory = draw_memory(jax.random.fold_in(arg_keys[9], 71), 0)
    near_device_keys = jax.random.split(jax.random.fold_in(arg_keys[5], 1), BLOCKS // BLK_DEV)
    near_device_turns = jax.random.permutation(jax.random.fold_in(arg_keys[5], 3), BLOCKS // BLK_DEV)
    near_device = jax.vmap(lambda own, number: shared_out(jax.random.fold_in(arg_keys[5], 2), own, number, BLK_DEV, N_SEQ, NEAR, CAP, 2))(near_device_keys, near_device_turns).reshape((BLOCKS, NEAR))
    near_slot = plant(jax.random.randint(arg_keys[6], (BLOCKS, NEAR), 0, BLK_DEV), jax.random.fold_in(arg_keys[6], 1), 0, BLK_DEV - 1).astype(jnp.int32)
    near_count = uneven_parts(arg_keys[7], BLOCKS, BLOCKS * (NEAR + 1) // 2, NEAR, 2).astype(jnp.int32)
    writer_block = draw_writer_block(jax.random.fold_in(arg_keys[9], 71), 0)
    return dict(queries=queries, key_states=key_states, value_states=value_states, out_grad=out_grad, memory=memory, near_device=near_device, near_slot=near_slot, near_count=near_count, writer_block=writer_block)


def rounded_width(value):
    return lax.optimization_barrier(value.astype(jnp.bfloat16))

def reference(queries, key_states, value_states, out_grad, memory, near_device, near_slot, near_count, writer_block):
    key_scaling_factor = 1.0 / math.sqrt(HD)
    block_scale = 1.0 / math.sqrt(BLK)
    near_block = (near_device * BLK_DEV + near_slot).astype(jnp.int32)

    def one_batch(inputs):
        query_rows, key_rows, value_rows, grad_rows = inputs
        value_sums = lax.optimization_barrier(jnp.sum(value_rows.reshape(BLOCKS, BLK, HW).astype(jnp.float32), axis=1))
        memory_keys = rounded_width(memory + value_sums[writer_block] * block_scale)
        memory_head_states = memory_keys.astype(jnp.float32).reshape(MEM, HEADS, HD)
        key_blocks = key_rows.reshape(BLOCKS, BLK, HW)
        value_blocks = value_rows.reshape(BLOCKS, BLK, HW)

        def one_block(grad_total, block_index):
            start = (block_index * BLK).astype(jnp.int32)
            query_head_states = lax.dynamic_slice_in_dim(query_rows, start, BLK, 0).astype(jnp.float32).reshape(BLK, HEADS, HD)
            head_output_gradient = lax.dynamic_slice_in_dim(grad_rows, start, BLK, 0).astype(jnp.float32).reshape(BLK, HEADS, HD)
            chosen = near_block[block_index]
            neighbour_key_rows = jnp.take(key_blocks, chosen, axis=0).astype(jnp.float32).reshape(NEAR * BLK, HEADS, HD)
            neighbour_value_rows = jnp.take(value_blocks, chosen, axis=0).astype(jnp.float32).reshape(NEAR * BLK, HEADS, HD)
            live_keys = jnp.arange(NEAR * BLK, dtype=jnp.int32) // BLK < near_count[block_index]
            memory_score_logits = jnp.einsum('lan,san->als', query_head_states, memory_head_states) * key_scaling_factor
            score_near = jnp.einsum('qhd,khd->hqk', query_head_states, neighbour_key_rows) * key_scaling_factor
            score_near = jnp.where(live_keys[None, None, :], score_near, -jnp.inf)
            row_max = jnp.maximum(lax.optimization_barrier(jnp.max(memory_score_logits, axis=-1)), lax.optimization_barrier(jnp.max(score_near, axis=-1)))
            exp_mem = jnp.exp(memory_score_logits - row_max[:, :, None])
            exp_near = jnp.exp(score_near - row_max[:, :, None])
            row_total = lax.optimization_barrier(jnp.sum(exp_mem, axis=-1)) + lax.optimization_barrier(jnp.sum(exp_near, axis=-1))
            prob_mem = exp_mem / row_total[:, :, None]
            prob_near = exp_near / row_total[:, :, None]
            memory_attention_weight = rounded_width(prob_mem).astype(jnp.float32)
            neighbour_attention_weight = rounded_width(prob_near).astype(jnp.float32)
            head_attended_output = rounded_width(jnp.einsum('ywo,oya->wya', memory_attention_weight, memory_head_states) + jnp.einsum('wpg,gwm->pwm', neighbour_attention_weight, neighbour_value_rows))
            grad_dot = lax.optimization_barrier(jnp.sum(head_output_gradient * head_attended_output.astype(jnp.float32), axis=-1)).T
            memory_probability_gradient = jnp.einsum('lan,san->als', head_output_gradient, memory_head_states)
            dprob_near = jnp.einsum('qhd,khd->hqk', head_output_gradient, neighbour_value_rows)
            memory_score_gradient = rounded_width(prob_mem * (memory_probability_gradient - grad_dot[:, :, None])).astype(jnp.float32)
            neighbour_score_gradient = rounded_width(prob_near * (dprob_near - grad_dot[:, :, None])).astype(jnp.float32)
            query_portion = rounded_width((jnp.einsum('ywo,oya->wya', memory_score_gradient, memory_head_states) + jnp.einsum('wpg,gwm->pwm', neighbour_score_gradient, neighbour_key_rows)) * key_scaling_factor)
            memory_contribution = jnp.einsum('toi,otl->itl', memory_score_gradient, query_head_states) * key_scaling_factor + jnp.einsum('toi,otl->itl', memory_attention_weight, head_output_gradient)
            key_parts = rounded_width(jnp.einsum('hqk,qhd->khd', neighbour_score_gradient, query_head_states) * key_scaling_factor).reshape(NEAR, BLK, HW)
            value_parts = rounded_width(jnp.einsum('hqk,qhd->khd', neighbour_attention_weight, head_output_gradient)).reshape(NEAR, BLK, HW)
            outputs = (head_attended_output.reshape(BLK, HW), query_portion.reshape(BLK, HW), key_parts, value_parts)
            return (grad_total + memory_contribution.reshape(MEM, HW), outputs)
        start_total = jnp.zeros((MEM, HW), jnp.float32)
        row_grad, stacked = lax.scan(one_block, start_total, jnp.arange(BLOCKS, dtype=jnp.int32))
        attended_rows, query_rows_grad, key_parts, value_parts = stacked
        flat_blocks = near_block.reshape(BLOCKS * NEAR)
        key_sum = jnp.zeros((BLOCKS, BLK, HW), jnp.float32).at[flat_blocks].add(key_parts.reshape(BLOCKS * NEAR, BLK, HW).astype(jnp.float32))
        value_sum = jnp.zeros((BLOCKS, BLK, HW), jnp.float32).at[flat_blocks].add(value_parts.reshape(BLOCKS * NEAR, BLK, HW).astype(jnp.float32))
        spread = jax.ops.segment_sum(row_grad, writer_block, num_segments=BLOCKS) * block_scale
        key_out = key_sum.astype(jnp.bfloat16).reshape(SEQ, HW)
        value_out = (value_sum + spread[:, None, :]).astype(jnp.bfloat16).reshape(SEQ, HW)
        return (attended_rows.reshape(SEQ, HW), query_rows_grad.reshape(SEQ, HW), key_out, value_out, row_grad)
    attended, query_grad, key_grad, value_grad, row_grads = lax.map(one_batch, (queries, key_states, value_states, out_grad))
    return (attended, query_grad, key_grad, value_grad, lax.optimization_barrier(jnp.sum(row_grads, axis=0)))
```

```python
import functools
import math

import jax
import jax.numpy as jnp
from jax import lax
from jax.experimental import pallas as pl
from jax.experimental.pallas import tpu as pltpu
from jax.sharding import PartitionSpec as P

HEADS = 8
HD = 128
BLK = 128
MEM = 1024
GROUPS = 2
F32 = jnp.float32
BF16 = jnp.bfloat16


def dot_nt(a, b):
    return lax.dot_general(a, b, (((1,), (1,)), ((), ())), preferred_element_type=F32)


def dot_tn(a, b):
    return lax.dot_general(a, b, (((0,), (0,)), ((), ())), preferred_element_type=F32)


def dot_nn(a, b):
    return lax.dot_general(a, b, (((1,), (0,)), ((), ())), preferred_element_type=F32)


def head_kernel(
    near_width,
    dev_ref,
    slot_ref,
    count_ref,
    q_ref,
    g_ref,
    kv_ref,
    mem_ref,
    second_ref,
    att_ref,
    qg_ref,
    out_ref,
    spread_ref,
):
    tokens = q_ref.shape[0]
    blocks = tokens // BLK
    n = kv_ref.shape[0]
    rows_dev = MEM // n
    scale = 1.0 / math.sqrt(HD)
    block_scale = 1.0 / math.sqrt(BLK)
    to_exp2 = scale * math.log2(math.e)
    values = kv_ref[:, tokens:, :].astype(F32).reshape(n, blocks, BLK, HD)
    sums = jnp.sum(values, axis=2)
    second = second_ref[...].reshape(n, rows_dev, 1) > 0.5
    add = jnp.where(second, sums[:, 1:2, :], sums[:, 0:1, :])
    mem_keys = (mem_ref[...].reshape(n, rows_dev, HD) + add * block_scale).astype(BF16)
    mem_keys = mem_keys.reshape(MEM, HD)
    term = jnp.zeros((MEM, HD), F32)
    parts = []
    for l in range(blocks):
        rows = slice(l * BLK, (l + 1) * BLK)
        q = q_ref[rows, :]
        g = g_ref[rows, :]
        keys, vals = [], []
        for j in range(near_width):
            d, s = dev_ref[l, j], slot_ref[l, j]
            keys.append(kv_ref[d, pl.ds(pl.multiple_of(s * BLK, BLK), BLK), :])
            vals.append(kv_ref[d, pl.ds(pl.multiple_of(tokens + s * BLK, BLK), BLK), :])
        near_keys = jnp.concatenate(keys, axis=0)
        near_vals = jnp.concatenate(vals, axis=0)
        s_mem = dot_nt(q, mem_keys)
        s_near = dot_nt(q, near_keys)
        live = lax.broadcasted_iota(jnp.int32, s_near.shape, 1) < count_ref[l] * BLK
        s_near = jnp.where(live, s_near, -jnp.inf)
        top = jnp.maximum(
            jnp.max(s_mem, axis=1, keepdims=True), jnp.max(s_near, axis=1, keepdims=True)
        )
        e_mem = jnp.exp2((s_mem - top) * to_exp2)
        e_near = jnp.exp2((s_near - top) * to_exp2)
        total = jnp.sum(e_mem, axis=1, keepdims=True) + jnp.sum(e_near, axis=1, keepdims=True)
        inv = 1.0 / total
        p_mem = e_mem * inv
        p_near = e_near * inv
        w_mem = p_mem.astype(BF16)
        w_near = p_near.astype(BF16)
        att = (dot_nn(w_mem, mem_keys) + dot_nn(w_near, near_vals)).astype(BF16)
        att_ref[rows, :] = att
        gdot = jnp.sum(g.astype(F32) * att.astype(F32), axis=1, keepdims=True)
        ds_mem = (p_mem * (dot_nt(g, mem_keys) - gdot)).astype(BF16)
        ds_near = (p_near * (dot_nt(g, near_vals) - gdot)).astype(BF16)
        qg_ref[rows, :] = (
            (dot_nn(ds_mem, mem_keys) + dot_nn(ds_near, near_keys)) * scale
        ).astype(BF16)
        term = term + dot_tn(ds_mem, q) * scale + dot_tn(w_mem, g)
        parts.append((dot_tn(ds_near, q) * scale, dot_tn(w_near, g)))
    rows3 = term.reshape(n, rows_dev, HD)
    first_sum = jnp.sum(jnp.where(second, 0.0, rows3), axis=1, keepdims=True) * block_scale
    second_sum = jnp.sum(jnp.where(second, rows3, 0.0), axis=1, keepdims=True) * block_scale
    spread = jnp.concatenate([first_sum, second_sum], axis=1)
    spread_ref[...] = spread
    out_ref[:, 0:tokens, :] = jnp.zeros((n, tokens, HD), BF16)
    for s in range(blocks):
        out_ref[:, tokens + s * BLK : tokens + (s + 1) * BLK, :] = jnp.broadcast_to(
            spread[:, s : s + 1, :], (n, BLK, HD)
        ).astype(BF16)
    out_ref[:, 2 * tokens :, :] = rows3.astype(BF16)
    for l in range(blocks):
        for j in range(near_width):
            d, s = dev_ref[l, j], slot_ref[l, j]
            here = slice(j * BLK, (j + 1) * BLK)
            row = spread_ref[d, pl.ds(s, 1), :]
            out_ref[d, pl.ds(pl.multiple_of(s * BLK, BLK), BLK), :] = parts[l][0][here].astype(BF16)
            out_ref[d, pl.ds(pl.multiple_of(tokens + s * BLK, BLK), BLK), :] = (
                parts[l][1][here] + row
            ).astype(BF16)


def attend_group(group, heads, tables, queries, out_grad, kv, memory, second):
    tokens = queries.shape[0]
    n = kv.shape[0]
    near_width = tables[0].shape[1]
    rows_dev = MEM // n
    first = group * heads
    width = heads * HD
    whole = lambda h, *_: (0, first + h)
    part = lambda h, *_: (0, h)
    part3 = lambda h, *_: (0, 0, h)
    keys = MEM + near_width * BLK
    return pl.pallas_call(
        functools.partial(head_kernel, near_width),
        out_shape=(
            jax.ShapeDtypeStruct((tokens, width), BF16),
            jax.ShapeDtypeStruct((tokens, width), BF16),
            jax.ShapeDtypeStruct((n, 2 * tokens + rows_dev, width), BF16),
        ),
        grid_spec=pltpu.PrefetchScalarGridSpec(
            num_scalar_prefetch=3,
            grid=(heads,),
            in_specs=[
                pl.BlockSpec((tokens, HD), whole),
                pl.BlockSpec((tokens, HD), whole),
                pl.BlockSpec((n, 2 * tokens, HD), part3),
                pl.BlockSpec((MEM, HD), whole),
                pl.BlockSpec((MEM, 1), lambda h, *_: (0, 0)),
            ],
            out_specs=(
                pl.BlockSpec((tokens, HD), part),
                pl.BlockSpec((tokens, HD), part),
                pl.BlockSpec((n, 2 * tokens + rows_dev, HD), part3),
            ),
            scratch_shapes=[pltpu.VMEM((n, tokens // BLK, HD), F32)],
        ),
        compiler_params=pltpu.CompilerParams(
            dimension_semantics=("arbitrary",), vmem_limit_bytes=50 * 1024 * 1024
        ),
        cost_estimate=pl.CostEstimate(
            flops=12 * tokens * keys * width,
            bytes_accessed=n * tokens * width * 10,
            transcendentals=heads * tokens * keys,
        ),
    )(*tables, queries, out_grad, kv, memory, second)


def shards(
    queries,
    key_states,
    value_states,
    out_grad,
    memory,
    near_device,
    near_slot,
    near_count,
    writer_block,
):
    my_index = lax.axis_index("seq")
    tokens = queries.shape[1]
    local_blocks = tokens // BLK
    heads = HEADS // GROUPS
    width = heads * HD
    mine = lambda t: lax.dynamic_slice_in_dim(t, my_index * local_blocks, local_blocks, 0)
    tables = (mine(near_device), mine(near_slot), mine(near_count))
    second = (writer_block % local_blocks).astype(F32).reshape(MEM, 1)
    gathered = []
    for group in range(GROUPS):
        cols = slice(group * width, (group + 1) * width)
        packed = jnp.concatenate([key_states[0][:, cols], value_states[0][:, cols]], axis=0)
        gathered.append(lax.all_gather(packed, "seq", axis=0, tiled=False))
    results = []
    for group in range(GROUPS):
        att, qg, out = attend_group(
            group, heads, tables, queries[0], out_grad[0], gathered[group], memory, second
        )
        got = lax.psum_scatter(out, "seq", scatter_dimension=0, tiled=False)
        results.append((att, qg, got[:tokens], got[tokens : 2 * tokens], got[2 * tokens :]))
    att, qg, kg, vg, rows = [jnp.concatenate(c, axis=1) for c in zip(*results)]
    memory_grad = lax.psum(rows, "batch").astype(F32)
    return (att[None], qg[None], kg[None], vg[None], memory_grad)


def solution(mesh):
    placed = (P("batch", "seq", None),) * 4 + (P(),) * 5
    return jax.shard_map(
        shards,
        mesh=mesh,
        in_specs=placed,
        out_specs=(P("batch", "seq", None),) * 4 + (P("seq", None),),
        check_vma=False,
    )
```

```python
import functools
import math

import jax
import jax.numpy as jnp
from jax import lax
from jax.experimental import pallas as pl
from jax.experimental.pallas import tpu as pltpu
from jax.sharding import PartitionSpec as P

HEADS = 8
HD = 128
BLK = 128
MEM = 1024
GROUPS = 2
F32 = jnp.float32
BF16 = jnp.bfloat16


def dot_nt(a, b):
    return lax.dot_general(a, b, (((1,), (1,)), ((), ())), preferred_element_type=F32)


def dot_tn(a, b):
    return lax.dot_general(a, b, (((0,), (0,)), ((), ())), preferred_element_type=F32)


def dot_nn(a, b):
    return lax.dot_general(a, b, (((1,), (0,)), ((), ())), preferred_element_type=F32)


def head_kernel(
    near_width,
    dev_ref,
    slot_ref,
    count_ref,
    q_ref,
    g_ref,
    kv_ref,
    mem_ref,
    second_ref,
    att_ref,
    qg_ref,
    out_ref,
    spread_ref,
):
    tokens = q_ref.shape[0]
    blocks = tokens // BLK
    n = kv_ref.shape[0]
    rows_dev = MEM // n
    scale = 1.0 / math.sqrt(HD)
    block_scale = 1.0 / math.sqrt(BLK)
    to_exp2 = scale * math.log2(math.e)
    values = kv_ref[:, tokens:, :].astype(F32).reshape(n, blocks, BLK, HD)
    sums = jnp.sum(values, axis=2)
    second = second_ref[...].reshape(n, rows_dev, 1) > 0.5
    add = jnp.where(second, sums[:, 1:2, :], sums[:, 0:1, :])
    mem_keys = (mem_ref[...].reshape(n, rows_dev, HD) + add * block_scale).astype(BF16)
    mem_keys = mem_keys.reshape(MEM, HD)
    term = jnp.zeros((MEM, HD), F32)
    parts = []
    for l in range(blocks):
        rows = slice(l * BLK, (l + 1) * BLK)
        q = q_ref[rows, :]
        g = g_ref[rows, :]
        keys, vals = [], []
        for j in range(near_width):
            d, s = dev_ref[l, j], slot_ref[l, j]
            keys.append(kv_ref[d, pl.ds(pl.multiple_of(s * BLK, BLK), BLK), :])
            vals.append(kv_ref[d, pl.ds(pl.multiple_of(tokens + s * BLK, BLK), BLK), :])
        near_keys = jnp.concatenate(keys, axis=0)
        near_vals = jnp.concatenate(vals, axis=0)
        s_mem = dot_nt(q, mem_keys)
        s_near = dot_nt(q, near_keys)
        live = lax.broadcasted_iota(jnp.int32, s_near.shape, 1) < count_ref[l] * BLK
        s_near = jnp.where(live, s_near, -jnp.inf)
        top = jnp.maximum(
            jnp.max(s_mem, axis=1, keepdims=True), jnp.max(s_near, axis=1, keepdims=True)
        )
        e_mem = jnp.exp2((s_mem - top) * to_exp2)
        e_near = jnp.exp2((s_near - top) * to_exp2)
        total = jnp.sum(e_mem, axis=1, keepdims=True) + jnp.sum(e_near, axis=1, keepdims=True)
        inv = 1.0 / total
        p_mem = e_mem * inv
        p_near = e_near * inv
        w_mem = p_mem.astype(BF16)
        w_near = p_near.astype(BF16)
        att = (dot_nn(w_mem, mem_keys) + dot_nn(w_near, near_vals)).astype(BF16)
        att_ref[rows, :] = att
        gdot = jnp.sum(g.astype(F32) * att.astype(F32), axis=1, keepdims=True)
        ds_mem = (p_mem * (dot_nt(g, mem_keys) - gdot)).astype(BF16)
        ds_near = (p_near * (dot_nt(g, near_vals) - gdot)).astype(BF16)
        qg_ref[rows, :] = (
            (dot_nn(ds_mem, mem_keys) + dot_nn(ds_near, near_keys)) * scale
        ).astype(BF16)
        term = term + dot_tn(ds_mem, q) * scale + dot_tn(w_mem, g)
        parts.append((dot_tn(ds_near, q) * scale, dot_tn(w_near, g)))
    rows3 = term.reshape(n, rows_dev, HD)
    first_sum = jnp.sum(jnp.where(second, 0.0, rows3), axis=1, keepdims=True) * block_scale
    second_sum = jnp.sum(jnp.where(second, rows3, 0.0), axis=1, keepdims=True) * block_scale
    spread = jnp.concatenate([first_sum, second_sum], axis=1)
    spread_ref[...] = spread
    out_ref[:, 0:tokens, :] = jnp.zeros((n, tokens, HD), BF16)
    for s in range(blocks):
        out_ref[:, tokens + s * BLK : tokens + (s + 1) * BLK, :] = jnp.broadcast_to(
            spread[:, s : s + 1, :], (n, BLK, HD)
        ).astype(BF16)
    out_ref[:, 2 * tokens :, :] = rows3.astype(BF16)
    for l in range(blocks):
        for j in range(near_width):
            d, s = dev_ref[l, j], slot_ref[l, j]
            here = slice(j * BLK, (j + 1) * BLK)
            row = spread_ref[d, pl.ds(s, 1), :]
            out_ref[d, pl.ds(pl.multiple_of(s * BLK, BLK), BLK), :] = parts[l][0][here].astype(BF16)
            out_ref[d, pl.ds(pl.multiple_of(tokens + s * BLK, BLK), BLK), :] = (
                parts[l][1][here] + row
            ).astype(BF16)


def attend_group(group, heads, tables, queries, out_grad, kv, memory, second):
    tokens = queries.shape[0]
    n = kv.shape[0]
    near_width = tables[0].shape[1]
    rows_dev = MEM // n
    first = group * heads
    width = heads * HD
    whole = lambda h, *_: (0, first + h)
    part = lambda h, *_: (0, h)
    part3 = lambda h, *_: (0, 0, h)
    keys = MEM + near_width * BLK
    return pl.pallas_call(
        functools.partial(head_kernel, near_width),
        out_shape=(
            jax.ShapeDtypeStruct((tokens, width), BF16),
            jax.ShapeDtypeStruct((tokens, width), BF16),
            jax.ShapeDtypeStruct((n, 2 * tokens + rows_dev, width), BF16),
        ),
        grid_spec=pltpu.PrefetchScalarGridSpec(
            num_scalar_prefetch=3,
            grid=(heads,),
            in_specs=[
                pl.BlockSpec((tokens, HD), whole),
                pl.BlockSpec((tokens, HD), whole),
                pl.BlockSpec((n, 2 * tokens, HD), part3),
                pl.BlockSpec((MEM, HD), whole),
                pl.BlockSpec((MEM, 1), lambda h, *_: (0, 0)),
            ],
            out_specs=(
                pl.BlockSpec((tokens, HD), part),
                pl.BlockSpec((tokens, HD), part),
                pl.BlockSpec((n, 2 * tokens + rows_dev, HD), part3),
            ),
            scratch_shapes=[pltpu.VMEM((n, tokens // BLK, HD), F32)],
        ),
        compiler_params=pltpu.CompilerParams(
            dimension_semantics=("arbitrary",), vmem_limit_bytes=50 * 1024 * 1024
        ),
        cost_estimate=pl.CostEstimate(
            flops=12 * tokens * keys * width,
            bytes_accessed=n * tokens * width * 10,
            transcendentals=heads * tokens * keys,
        ),
    )(*tables, queries, out_grad, kv, memory, second)


def shards(
    queries,
    key_states,
    value_states,
    out_grad,
    memory,
    near_device,
    near_slot,
    near_count,
    writer_block,
):
    my_index = lax.axis_index("seq")
    tokens = queries.shape[1]
    local_blocks = tokens // BLK
    heads = HEADS // GROUPS
    width = heads * HD
    mine = lambda t: lax.dynamic_slice_in_dim(t, my_index * local_blocks, local_blocks, 0)
    tables = (mine(near_device), mine(near_slot), mine(near_count))
    second = (writer_block % local_blocks).astype(F32).reshape(MEM, 1)
    gathered = []
    for group in range(GROUPS):
        cols = slice(group * width, (group + 1) * width)
        packed = jnp.concatenate([key_states[0][:, cols], value_states[0][:, cols]], axis=0)
        gathered.append(lax.all_gather(packed, "seq", axis=0, tiled=False))
    results = []
    for group in range(GROUPS):
        att, qg, out = attend_group(
            group, heads, tables, queries[0], out_grad[0], gathered[group], memory, second
        )
        got = lax.psum_scatter(out, "seq", scatter_dimension=0, tiled=False)
        results.append((att, qg, got[:tokens], got[tokens : 2 * tokens], got[2 * tokens :]))
    att, qg, kg, vg, rows = [jnp.concatenate(c, axis=1) for c in zip(*results)]
    memory_grad = lax.psum(rows, "batch").astype(F32)
    return (att[None], qg[None], kg[None], vg[None], memory_grad)


MESH = pl.DeviceIdType.MESH


def fused_kernel(
    lines,
    peers,
    q_ref,
    k_ref,
    v_ref,
    g_ref,
    mem_ref,
    second_ref,
    bias_ref,
    slot_ref,
    att_ref,
    qg_ref,
    kg_ref,
    vg_ref,
    mg_ref,
    kv,
    own,
    sib,
    ups,
    downs,
    rows_own,
    rows_got,
    up_send,
    down_send,
    share_send,
    kv_recv,
    sib_send,
    sib_recv,
    ups_send,
    ups_recv,
    downs_send,
    downs_recv,
    rows_send,
    rows_recv,
):
    n = 2 * lines
    tokens = q_ref.shape[0]
    rows_dev = MEM // n
    scale = 1.0 / math.sqrt(HD)
    block_scale = 1.0 / math.sqrt(BLK)
    to_exp2 = scale * math.log2(math.e)
    me = lax.axis_index("seq")
    b = lax.axis_index("batch")
    z, core = me // 2, me % 2
    last = lines - 1

    def at(zz, cc):
        return (b, zz * 2 + cc)

    barrier = pltpu.get_barrier_semaphore()

    @pl.when(z < last)
    def _():
        pl.semaphore_signal(barrier, inc=1, device_id=at(z + 1, core), device_id_type=MESH)

    @pl.when(z > 0)
    def _():
        pl.semaphore_signal(barrier, inc=1, device_id=at(z - 1, core), device_id_type=MESH)

    pl.semaphore_signal(barrier, inc=1, device_id=at(z, 1 - core), device_id_type=MESH)
    for p in range(1, peers):
        pl.semaphore_signal(barrier, inc=1, device_id=((b + p) % peers, me), device_id_type=MESH)
    edges = jnp.where(z < last, 1, 0) + jnp.where(z > 0, 1, 0)
    pl.semaphore_wait(barrier, edges + peers)

    def send(src, dst, s, r, dev):
        return pltpu.make_async_remote_copy(
            src_ref=src, dst_ref=dst, send_sem=s, recv_sem=r, device_id=dev, device_id_type=MESH
        )

    def kv_up(h, o):
        i = o * 2 + core
        return send(
            kv.at[h, i], kv.at[h, i], up_send.at[h, o], kv_recv.at[h, i], at((z + 1) % lines, core)
        )

    def kv_down(h, o):
        i = o * 2 + core
        return send(
            kv.at[h, i],
            kv.at[h, i],
            down_send.at[h, o],
            kv_recv.at[h, i],
            at((z + last) % lines, core),
        )

    def kv_share(h, o):
        i = o * 2 + core
        return send(
            kv.at[h, i], kv.at[h, i], share_send.at[h, o], kv_recv.at[h, i], at(z, 1 - core)
        )

    def kv_got(h, o, c):
        i = o * 2 + c
        send(
            kv.at[h, i], kv.at[h, i], share_send.at[h, o], kv_recv.at[h, i], at(z, 1 - core)
        ).wait_recv()

    def sib_copy(h):
        return send(own.at[h, 1 - core], sib.at[h], sib_send.at[h], sib_recv.at[h], at(z, 1 - core))

    def sum_up(h, d):
        return send(
            own.at[h, core, d],
            ups.at[h, d],
            ups_send.at[h, d],
            ups_recv.at[h, d],
            at((z + 1) % lines, core),
        )

    def sum_down(h, d):
        return send(
            own.at[h, core, d],
            downs.at[h, d],
            downs_send.at[h, d],
            downs_recv.at[h, d],
            at((z + last) % lines, core),
        )

    def row_copy(h, p):
        return send(
            rows_own.at[h],
            rows_got.at[h, p],
            rows_send.at[h, p],
            rows_recv.at[h, p],
            ((b + p + 1) % peers, me),
        )

    def lanes(h):
        return pl.ds(pl.multiple_of(h * HD, HD), HD)

    def gather_first(h):
        kv[h, me, 0:tokens, :] = k_ref[:, lanes(h)]
        kv[h, me, tokens : 2 * tokens, :] = v_ref[:, lanes(h)]

        @pl.when(z < last)
        def _():
            kv_up(h, z).start()

        @pl.when(z > 0)
        def _():
            kv_down(h, z).start()

        kv_share(h, z).start()

    def gather_next(h, k):
        @pl.when(z >= k)
        def _():
            kv_got(h, z - k, core)

            @pl.when(z < last)
            def _():
                kv_up(h, z - k).start()

            kv_share(h, z - k).start()

        @pl.when(z + k <= last)
        def _():
            kv_got(h, z + k, core)

            @pl.when(z > 0)
            def _():
                kv_down(h, z + k).start()

            kv_share(h, z + k).start()

    def compute(h):
        for o in range(lines):
            kv_got(h, o, 1 - core)
        q = q_ref[:, lanes(h)]
        g = g_ref[:, lanes(h)]
        values = kv[h, :, tokens:, :].astype(F32).reshape(n, 2, BLK, HD)
        sums = jnp.sum(values, axis=2)
        second = second_ref[...].reshape(n, rows_dev, 1) > 0.5
        add = jnp.where(second, sums[:, 1:2, :], sums[:, 0:1, :])
        mem_keys = (mem_ref[:, lanes(h)].reshape(n, rows_dev, HD) + add * block_scale).astype(BF16)
        mem_keys = mem_keys.reshape(MEM, HD)
        keys, vals = [], []
        for d in range(n):
            pick = slot_ref[d : d + 1, :] > 0.5
            pair = lambda start: jnp.where(
                pick,
                kv[h, d, start + BLK : start + 2 * BLK, :].astype(F32),
                kv[h, d, start : start + BLK, :].astype(F32),
            ).astype(BF16)
            keys.append(pair(0))
            vals.append(pair(tokens))
        near_keys = jnp.concatenate(keys, axis=0)
        near_vals = jnp.concatenate(vals, axis=0)
        bias = jnp.concatenate(
            [jnp.broadcast_to(bias_ref[l : l + 1, :], (BLK, n * BLK)) for l in range(2)], axis=0
        )
        s_mem = dot_nt(q, mem_keys)
        s_near = dot_nt(q, near_keys) + bias
        top = jnp.maximum(
            jnp.max(s_mem, axis=1, keepdims=True), jnp.max(s_near, axis=1, keepdims=True)
        )
        e_mem = jnp.exp2((s_mem - top) * to_exp2)
        e_near = jnp.exp2((s_near - top) * to_exp2)
        inv = 1.0 / (
            jnp.sum(e_mem, axis=1, keepdims=True) + jnp.sum(e_near, axis=1, keepdims=True)
        )
        p_mem = e_mem * inv
        p_near = e_near * inv
        w_mem = p_mem.astype(BF16)
        w_near = p_near.astype(BF16)
        att = (dot_nn(w_mem, mem_keys) + dot_nn(w_near, near_vals)).astype(BF16)
        att_ref[:, lanes(h)] = att
        gdot = jnp.sum(g.astype(F32) * att.astype(F32), axis=1, keepdims=True)
        ds_mem = (p_mem * (dot_nt(g, mem_keys) - gdot)).astype(BF16)
        ds_near = (p_near * (dot_nt(g, near_vals) - gdot)).astype(BF16)
        qg_ref[:, lanes(h)] = (
            (dot_nn(ds_mem, mem_keys) + dot_nn(ds_near, near_keys)) * scale
        ).astype(BF16)
        rows3 = (dot_tn(ds_mem, q) * scale + dot_tn(w_mem, g)).reshape(n, rows_dev, HD)
        first_sum = jnp.sum(jnp.where(second, 0.0, rows3), axis=1, keepdims=True) * block_scale
        second_sum = jnp.sum(jnp.where(second, rows3, 0.0), axis=1, keepdims=True) * block_scale
        key_part = dot_tn(ds_near, q) * scale
        value_part = dot_tn(w_near, g)
        for d in range(n):
            here = slice(d * BLK, (d + 1) * BLK)
            pick = slot_ref[d : d + 1, :] > 0.5
            dk, dv = key_part[here], value_part[here]
            dz, dc = d // 2, d % 2
            own[h, dc, dz, 0:BLK, :] = jnp.where(pick, 0.0, dk).astype(BF16)
            own[h, dc, dz, BLK : 2 * BLK, :] = jnp.where(pick, dk, 0.0).astype(BF16)
            own[h, dc, dz, tokens : tokens + BLK, :] = (
                jnp.where(pick, 0.0, dv) + first_sum[d]
            ).astype(BF16)
            own[h, dc, dz, tokens + BLK : 2 * tokens, :] = (
                jnp.where(pick, dv, 0.0) + second_sum[d]
            ).astype(BF16)
            own[h, dc, dz, 2 * tokens :, :] = rows3[d].astype(BF16)
        sib_copy(h).start()

    def plus(a, c):
        return a.astype(F32) + c.astype(F32)

    def send_up(h, zz):
        @pl.when(z == zz)
        def _():
            for d in range(zz + 1, lines):
                sum_up(h, d).start()

    def send_down(h, zz):
        @pl.when(z == zz)
        def _():
            for d in range(zz):
                sum_down(h, d).start()

    def sum_first(h):
        sib_copy(h).wait_recv()
        own[h, core] = plus(own[h, core], sib[h]).astype(BF16)
        send_up(h, 0)
        send_down(h, last)

    def sum_next(h, k):
        @pl.when(z == k)
        def _():
            for d in range(k + 1, lines):
                sum_up(h, d).wait_recv()
                own[h, core, d] = plus(own[h, core, d], ups[h, d]).astype(BF16)
                sum_up(h, d).start()

        @pl.when(z == last - k)
        def _():
            for d in range(last - k):
                sum_down(h, d).wait_recv()
                own[h, core, d] = plus(own[h, core, d], downs[h, d]).astype(BF16)
                sum_down(h, d).start()

    def write_sums(h, total):
        kg_ref[:, lanes(h)] = total[0:tokens].astype(BF16)
        vg_ref[:, lanes(h)] = total[tokens : 2 * tokens].astype(BF16)
        rows_own[h] = total[2 * tokens :].astype(BF16)

    def finish(h):
        @pl.when(z > 0)
        def _():
            sum_up(h, z).wait_recv()

        @pl.when(z < last)
        def _():
            sum_down(h, z).wait_recv()

        @pl.when(z == 0)
        def _():
            write_sums(h, plus(own[h, core, 0], downs[h, 0]))

        @pl.when(z == last)
        def _():
            write_sums(h, plus(own[h, core, last], ups[h, last]))

        @pl.when(jnp.logical_and(z > 0, z < last))
        def _():
            write_sums(h, plus(own[h, core, z], ups[h, z]) + downs[h, z].astype(F32))

        for p in range(peers - 1):
            row_copy(h, p).start()

    def write_rows(h):
        total = rows_own[h].astype(F32)
        for p in range(peers - 1):
            row_copy(h, p).wait_recv()
            total = total + rows_got[h, p].astype(F32)
        mg_ref[:, lanes(h)] = total

    stages = [(0, gather_first)]
    for k in range(1, lines):
        stages.append((k, functools.partial(gather_next, k=k)))
    stages.append((lines + 1, sum_first))
    for k in range(1, last):
        stages.append((lines + 1 + k, functools.partial(sum_next, k=k)))
    stages.append((2 * lines, finish))
    stages.append((2 * lines + 1, write_rows))
    stages.append((lines, compute))

    def tick(t, carry):
        for lag, stage in stages:

            @pl.when(jnp.logical_and(t >= lag, t < HEADS + lag))
            def _(lag=lag, stage=stage):
                stage(t - lag)

        return carry

    lax.fori_loop(0, HEADS + 2 * lines + 2, tick, 0)

    def drain(h, carry):
        for o in range(lines):
            kv_share(h, o).wait_send()

            @pl.when(jnp.logical_and(z < last, o <= z))
            def _(o=o):
                kv_up(h, o).wait_send()

            @pl.when(jnp.logical_and(z > 0, o >= z))
            def _(o=o):
                kv_down(h, o).wait_send()

            @pl.when(o > z)
            def _(o=o):
                sum_up(h, o).wait_send()

            @pl.when(o < z)
            def _(o=o):
                sum_down(h, o).wait_send()

        sib_copy(h).wait_send()
        for p in range(peers - 1):
            row_copy(h, p).wait_send()
        return carry

    lax.fori_loop(0, HEADS, drain, 0)


def fused(
    queries,
    key_states,
    value_states,
    out_grad,
    memory,
    near_device,
    near_slot,
    near_count,
    writer_block,
):
    me = lax.axis_index("seq")
    n = lax.axis_size("seq")
    peers = lax.axis_size("batch")
    lines = n // 2
    tokens = queries.shape[1]
    width = queries.shape[2]
    near_width = near_device.shape[1]
    rows_dev = MEM // n
    mine = lambda t: lax.dynamic_slice_in_dim(t, me * 2, 2, 0)
    device, slot, count = mine(near_device), mine(near_slot), mine(near_count)
    named = device[:, :, None] == jnp.arange(n)[None, None, :]
    alive = jnp.arange(near_width)[None, :] < count[:, None]
    live = jnp.any(jnp.logical_and(named, alive[:, :, None]), axis=1)
    bias = jnp.repeat(jnp.where(live, 0.0, -jnp.inf).astype(F32), BLK, axis=1)
    picked = jnp.sum(jnp.where(named, slot[:, :, None], 0), axis=(0, 1)).astype(F32)
    picked = jnp.broadcast_to(picked[:, None], (n, HD))
    second = (writer_block % 2).astype(F32).reshape(MEM, 1)
    pack = 2 * tokens + rows_dev
    dma = pltpu.SemaphoreType.DMA
    vmem = pl.BlockSpec(memory_space=pltpu.VMEM)
    outs = pl.pallas_call(
        functools.partial(fused_kernel, lines, peers),
        out_shape=[jax.ShapeDtypeStruct((tokens, width), BF16)] * 4
        + [jax.ShapeDtypeStruct((rows_dev, width), F32)],
        in_specs=[vmem] * 8,
        out_specs=[vmem] * 5,
        scratch_shapes=[
            pltpu.VMEM((HEADS, n, 2 * tokens, HD), BF16),
            pltpu.VMEM((HEADS, 2, lines, pack, HD), BF16),
            pltpu.VMEM((HEADS, lines, pack, HD), BF16),
            pltpu.VMEM((HEADS, lines, pack, HD), BF16),
            pltpu.VMEM((HEADS, lines, pack, HD), BF16),
            pltpu.VMEM((HEADS, rows_dev, HD), BF16),
            pltpu.VMEM((HEADS, peers - 1, rows_dev, HD), BF16),
            dma((HEADS, lines)),
            dma((HEADS, lines)),
            dma((HEADS, lines)),
            dma((HEADS, n)),
            dma((HEADS,)),
            dma((HEADS,)),
            dma((HEADS, lines)),
            dma((HEADS, lines)),
            dma((HEADS, lines)),
            dma((HEADS, lines)),
            dma((HEADS, peers - 1)),
            dma((HEADS, peers - 1)),
        ],
        compiler_params=pltpu.CompilerParams(
            collective_id=0, has_side_effects=True, vmem_limit_bytes=60 * 1024 * 1024
        ),
    )(
        queries[0],
        key_states[0],
        value_states[0],
        out_grad[0],
        memory,
        second,
        bias,
        picked,
    )
    return tuple(o[None] for o in outs[:4]) + (outs[4],)


def solution(mesh):
    placed = (P("batch", "seq", None),) * 4 + (P(),) * 5
    one_line = mesh.shape["seq"] == 8 and mesh.shape["batch"] == 4
    return jax.shard_map(
        fused if one_line else shards,
        mesh=mesh,
        in_specs=placed,
        out_specs=(P("batch", "seq", None),) * 4 + (P("seq", None),),
        check_vma=False,
    )
```

```python
import functools
import math

import jax
import jax.numpy as jnp
from jax import lax
from jax.experimental import pallas as pl
from jax.experimental.pallas import tpu as pltpu
from jax.sharding import PartitionSpec as P

HEADS = 8
HD = 128
BLK = 128
MEM = 1024
GROUPS = 2
F32 = jnp.float32
BF16 = jnp.bfloat16


def dot_nt(a, b):
    return lax.dot_general(a, b, (((1,), (1,)), ((), ())), preferred_element_type=F32)


def dot_tn(a, b):
    return lax.dot_general(a, b, (((0,), (0,)), ((), ())), preferred_element_type=F32)


def dot_nn(a, b):
    return lax.dot_general(a, b, (((1,), (0,)), ((), ())), preferred_element_type=F32)


def head_kernel(
    near_width,
    dev_ref,
    slot_ref,
    count_ref,
    q_ref,
    g_ref,
    kv_ref,
    mem_ref,
    second_ref,
    att_ref,
    qg_ref,
    out_ref,
    spread_ref,
):
    tokens = q_ref.shape[0]
    blocks = tokens // BLK
    n = kv_ref.shape[0]
    rows_dev = MEM // n
    scale = 1.0 / math.sqrt(HD)
    block_scale = 1.0 / math.sqrt(BLK)
    to_exp2 = scale * math.log2(math.e)
    values = kv_ref[:, tokens:, :].astype(F32).reshape(n, blocks, BLK, HD)
    sums = jnp.sum(values, axis=2)
    second = second_ref[...].reshape(n, rows_dev, 1) > 0.5
    add = jnp.where(second, sums[:, 1:2, :], sums[:, 0:1, :])
    mem_keys = (mem_ref[...].reshape(n, rows_dev, HD) + add * block_scale).astype(BF16)
    mem_keys = mem_keys.reshape(MEM, HD)
    term = jnp.zeros((MEM, HD), F32)
    parts = []
    for l in range(blocks):
        rows = slice(l * BLK, (l + 1) * BLK)
        q = q_ref[rows, :]
        g = g_ref[rows, :]
        keys, vals = [], []
        for j in range(near_width):
            d, s = dev_ref[l, j], slot_ref[l, j]
            keys.append(kv_ref[d, pl.ds(pl.multiple_of(s * BLK, BLK), BLK), :])
            vals.append(kv_ref[d, pl.ds(pl.multiple_of(tokens + s * BLK, BLK), BLK), :])
        near_keys = jnp.concatenate(keys, axis=0)
        near_vals = jnp.concatenate(vals, axis=0)
        s_mem = dot_nt(q, mem_keys)
        s_near = dot_nt(q, near_keys)
        live = lax.broadcasted_iota(jnp.int32, s_near.shape, 1) < count_ref[l] * BLK
        s_near = jnp.where(live, s_near, -jnp.inf)
        top = jnp.maximum(
            jnp.max(s_mem, axis=1, keepdims=True), jnp.max(s_near, axis=1, keepdims=True)
        )
        e_mem = jnp.exp2((s_mem - top) * to_exp2)
        e_near = jnp.exp2((s_near - top) * to_exp2)
        total = jnp.sum(e_mem, axis=1, keepdims=True) + jnp.sum(e_near, axis=1, keepdims=True)
        inv = 1.0 / total
        p_mem = e_mem * inv
        p_near = e_near * inv
        w_mem = p_mem.astype(BF16)
        w_near = p_near.astype(BF16)
        att = (dot_nn(w_mem, mem_keys) + dot_nn(w_near, near_vals)).astype(BF16)
        att_ref[rows, :] = att
        gdot = jnp.sum(g.astype(F32) * att.astype(F32), axis=1, keepdims=True)
        ds_mem = (p_mem * (dot_nt(g, mem_keys) - gdot)).astype(BF16)
        ds_near = (p_near * (dot_nt(g, near_vals) - gdot)).astype(BF16)
        qg_ref[rows, :] = (
            (dot_nn(ds_mem, mem_keys) + dot_nn(ds_near, near_keys)) * scale
        ).astype(BF16)
        term = term + dot_tn(ds_mem, q) * scale + dot_tn(w_mem, g)
        parts.append((dot_tn(ds_near, q) * scale, dot_tn(w_near, g)))
    rows3 = term.reshape(n, rows_dev, HD)
    first_sum = jnp.sum(jnp.where(second, 0.0, rows3), axis=1, keepdims=True) * block_scale
    second_sum = jnp.sum(jnp.where(second, rows3, 0.0), axis=1, keepdims=True) * block_scale
    spread = jnp.concatenate([first_sum, second_sum], axis=1)
    spread_ref[...] = spread
    out_ref[:, 0:tokens, :] = jnp.zeros((n, tokens, HD), BF16)
    for s in range(blocks):
        out_ref[:, tokens + s * BLK : tokens + (s + 1) * BLK, :] = jnp.broadcast_to(
            spread[:, s : s + 1, :], (n, BLK, HD)
        ).astype(BF16)
    out_ref[:, 2 * tokens :, :] = rows3.astype(BF16)
    for l in range(blocks):
        for j in range(near_width):
            d, s = dev_ref[l, j], slot_ref[l, j]
            here = slice(j * BLK, (j + 1) * BLK)
            row = spread_ref[d, pl.ds(s, 1), :]
            out_ref[d, pl.ds(pl.multiple_of(s * BLK, BLK), BLK), :] = parts[l][0][here].astype(BF16)
            out_ref[d, pl.ds(pl.multiple_of(tokens + s * BLK, BLK), BLK), :] = (
                parts[l][1][here] + row
            ).astype(BF16)


def attend_group(group, heads, tables, queries, out_grad, kv, memory, second):
    tokens = queries.shape[0]
    n = kv.shape[0]
    near_width = tables[0].shape[1]
    rows_dev = MEM // n
    first = group * heads
    width = heads * HD
    whole = lambda h, *_: (0, first + h)
    part = lambda h, *_: (0, h)
    part3 = lambda h, *_: (0, 0, h)
    keys = MEM + near_width * BLK
    return pl.pallas_call(
        functools.partial(head_kernel, near_width),
        out_shape=(
            jax.ShapeDtypeStruct((tokens, width), BF16),
            jax.ShapeDtypeStruct((tokens, width), BF16),
            jax.ShapeDtypeStruct((n, 2 * tokens + rows_dev, width), BF16),
        ),
        grid_spec=pltpu.PrefetchScalarGridSpec(
            num_scalar_prefetch=3,
            grid=(heads,),
            in_specs=[
                pl.BlockSpec((tokens, HD), whole),
                pl.BlockSpec((tokens, HD), whole),
                pl.BlockSpec((n, 2 * tokens, HD), part3),
                pl.BlockSpec((MEM, HD), whole),
                pl.BlockSpec((MEM, 1), lambda h, *_: (0, 0)),
            ],
            out_specs=(
                pl.BlockSpec((tokens, HD), part),
                pl.BlockSpec((tokens, HD), part),
                pl.BlockSpec((n, 2 * tokens + rows_dev, HD), part3),
            ),
            scratch_shapes=[pltpu.VMEM((n, tokens // BLK, HD), F32)],
        ),
        compiler_params=pltpu.CompilerParams(
            dimension_semantics=("arbitrary",), vmem_limit_bytes=50 * 1024 * 1024
        ),
        cost_estimate=pl.CostEstimate(
            flops=12 * tokens * keys * width,
            bytes_accessed=n * tokens * width * 10,
            transcendentals=heads * tokens * keys,
        ),
    )(*tables, queries, out_grad, kv, memory, second)


def shards(
    queries,
    key_states,
    value_states,
    out_grad,
    memory,
    near_device,
    near_slot,
    near_count,
    writer_block,
):
    my_index = lax.axis_index("seq")
    tokens = queries.shape[1]
    local_blocks = tokens // BLK
    heads = HEADS // GROUPS
    width = heads * HD
    mine = lambda t: lax.dynamic_slice_in_dim(t, my_index * local_blocks, local_blocks, 0)
    tables = (mine(near_device), mine(near_slot), mine(near_count))
    second = (writer_block % local_blocks).astype(F32).reshape(MEM, 1)
    gathered = []
    for group in range(GROUPS):
        cols = slice(group * width, (group + 1) * width)
        packed = jnp.concatenate([key_states[0][:, cols], value_states[0][:, cols]], axis=0)
        gathered.append(lax.all_gather(packed, "seq", axis=0, tiled=False))
    results = []
    for group in range(GROUPS):
        att, qg, out = attend_group(
            group, heads, tables, queries[0], out_grad[0], gathered[group], memory, second
        )
        got = lax.psum_scatter(out, "seq", scatter_dimension=0, tiled=False)
        results.append((att, qg, got[:tokens], got[tokens : 2 * tokens], got[2 * tokens :]))
    att, qg, kg, vg, rows = [jnp.concatenate(c, axis=1) for c in zip(*results)]
    memory_grad = lax.psum(rows, "batch").astype(F32)
    return (att[None], qg[None], kg[None], vg[None], memory_grad)


MESH = pl.DeviceIdType.MESH


def fused_kernel(
    lines,
    peers,
    q_ref,
    k_ref,
    v_ref,
    g_ref,
    mem_ref,
    writer_ref,
    bias_ref,
    slot_ref,
    att_ref,
    qg_ref,
    kg_ref,
    vg_ref,
    mg_ref,
    kv,
    own,
    sib,
    ups,
    downs,
    acc,
    tsum,
    tgot,
    second_mask,
    rows_own,
    rows_got,
    up_send,
    down_send,
    share_send,
    kv_recv,
    sib_send,
    sib_recv,
    ups_send,
    ups_recv,
    downs_send,
    downs_recv,
    tsum_send,
    tsum_recv,
    rows_send,
    rows_recv,
):
    n = 2 * lines
    tokens = q_ref.shape[0]
    rows_dev = MEM // n
    scale = 1.0 / math.sqrt(HD)
    block_scale = 1.0 / math.sqrt(BLK)
    to_exp2 = scale * math.log2(math.e)
    me = lax.axis_index("seq")
    b = lax.axis_index("batch")
    z, core = me // 2, me % 2
    last = lines - 1
    quarter = rows_dev // peers

    def at(zz, cc):
        return (b, zz * 2 + cc)

    barrier = pltpu.get_barrier_semaphore()

    @pl.when(z < last)
    def _():
        pl.semaphore_signal(barrier, inc=1, device_id=at(z + 1, core), device_id_type=MESH)

    @pl.when(z > 0)
    def _():
        pl.semaphore_signal(barrier, inc=1, device_id=at(z - 1, core), device_id_type=MESH)

    pl.semaphore_signal(barrier, inc=1, device_id=at(z, 1 - core), device_id_type=MESH)
    for p in range(1, peers):
        pl.semaphore_signal(barrier, inc=1, device_id=((b + p) % peers, me), device_id_type=MESH)
    edges = jnp.where(z < last, 1, 0) + jnp.where(z > 0, 1, 0)
    pl.semaphore_wait(barrier, edges + peers)

    def send(src, dst, s, r, dev):
        return pltpu.make_async_remote_copy(
            src_ref=src, dst_ref=dst, send_sem=s, recv_sem=r, device_id=dev, device_id_type=MESH
        )

    def kv_up(h, o):
        i = o * 2 + core
        return send(
            kv.at[h, i], kv.at[h, i], up_send.at[h, o], kv_recv.at[h, i], at((z + 1) % lines, core)
        )

    def kv_down(h, o):
        i = o * 2 + core
        return send(
            kv.at[h, i],
            kv.at[h, i],
            down_send.at[h, o],
            kv_recv.at[h, i],
            at((z + last) % lines, core),
        )

    def kv_share(h, o):
        i = o * 2 + core
        return send(
            kv.at[h, i], kv.at[h, i], share_send.at[h, o], kv_recv.at[h, i], at(z, 1 - core)
        )

    def kv_got(h, o, c):
        i = o * 2 + c
        send(
            kv.at[h, i], kv.at[h, i], share_send.at[h, o], kv_recv.at[h, i], at(z, 1 - core)
        ).wait_recv()

    def sib_copy(h):
        return send(own.at[h, 1 - core], sib.at[h], sib_send.at[h], sib_recv.at[h], at(z, 1 - core))

    def sum_up(h, d):
        return send(
            acc.at[h, d],
            ups.at[h, d],
            ups_send.at[h, d],
            ups_recv.at[h, d],
            at((z + 1) % lines, core),
        )

    def sum_down(h, d):
        return send(
            acc.at[h, d],
            downs.at[h, d],
            downs_send.at[h, d],
            downs_recv.at[h, d],
            at((z + last) % lines, core),
        )

    def row_copy(h, p):
        return send(
            rows_own.at[h],
            rows_got.at[h, p],
            rows_send.at[h, p],
            rows_recv.at[h, p],
            ((b + p + 1) % peers, me),
        )

    def part(p):
        return pl.ds(pl.multiple_of(p * quarter, quarter), quarter)

    def tsum_copy(h, p):
        peer = (b + p + 1) % peers
        return send(
            tsum.at[h, :, part(peer), :],
            tgot.at[h, p],
            tsum_send.at[h, p],
            tsum_recv.at[h, p],
            (peer, me),
        )

    for d in range(n):
        odd = (writer_ref[d : d + 1, :] % 2).astype(F32)
        second_mask[d] = jnp.broadcast_to(odd, (rows_dev, HD)).T

    def lanes(h):
        return pl.ds(pl.multiple_of(h * HD, HD), HD)

    def gather_first(h):
        kv[h, me, 0:tokens, :] = k_ref[:, lanes(h)]
        kv[h, me, tokens : 2 * tokens, :] = v_ref[:, lanes(h)]

        @pl.when(z < last)
        def _():
            kv_up(h, z).start()

        @pl.when(z > 0)
        def _():
            kv_down(h, z).start()

        kv_share(h, z).start()

    def gather_next(h, k):
        @pl.when(z >= k)
        def _():
            kv_got(h, z - k, core)

            @pl.when(z < last)
            def _():
                kv_up(h, z - k).start()

            kv_share(h, z - k).start()

        @pl.when(z + k <= last)
        def _():
            kv_got(h, z + k, core)

            @pl.when(z > 0)
            def _():
                kv_down(h, z + k).start()

            kv_share(h, z + k).start()

    def compute(h):
        for o in range(lines):
            kv_got(h, o, 1 - core)
        q = q_ref[:, lanes(h)]
        g = g_ref[:, lanes(h)]
        values = kv[h, :, tokens:, :].astype(F32).reshape(n, 2, BLK, HD)
        sums = jnp.sum(values, axis=2)
        second = second_mask[...] > 0.5
        add = jnp.where(second, sums[:, 1:2, :], sums[:, 0:1, :])
        mem_keys = (mem_ref[:, lanes(h)].reshape(n, rows_dev, HD) + add * block_scale).astype(BF16)
        mem_keys = mem_keys.reshape(MEM, HD)
        keys, vals = [], []
        for d in range(n):
            pick = slot_ref[d : d + 1, :] > 0.5
            pair = lambda start: jnp.where(
                pick,
                kv[h, d, start + BLK : start + 2 * BLK, :].astype(F32),
                kv[h, d, start : start + BLK, :].astype(F32),
            ).astype(BF16)
            keys.append(pair(0))
            vals.append(pair(tokens))
        near_keys = jnp.concatenate(keys, axis=0)
        near_vals = jnp.concatenate(vals, axis=0)
        bias = jnp.concatenate(
            [jnp.broadcast_to(bias_ref[l : l + 1, :], (BLK, n * BLK)) for l in range(2)], axis=0
        )
        s_mem = dot_nt(q, mem_keys)
        s_near = dot_nt(q, near_keys) + bias
        top = jnp.maximum(
            jnp.max(s_mem, axis=1, keepdims=True), jnp.max(s_near, axis=1, keepdims=True)
        )
        e_mem = jnp.exp2((s_mem - top) * to_exp2)
        e_near = jnp.exp2((s_near - top) * to_exp2)
        inv = 1.0 / (
            jnp.sum(e_mem, axis=1, keepdims=True) + jnp.sum(e_near, axis=1, keepdims=True)
        )
        p_mem = e_mem * inv
        p_near = e_near * inv
        w_mem = p_mem.astype(BF16)
        w_near = p_near.astype(BF16)
        att = (dot_nn(w_mem, mem_keys) + dot_nn(w_near, near_vals)).astype(BF16)
        att = att.astype(F32)
        att_ref[:, lanes(h)] = att
        gdot = jnp.sum(g.astype(F32) * att, axis=1, keepdims=True)
        ds_mem = (p_mem * (dot_nt(g, mem_keys) - gdot)).astype(BF16)
        ds_near = (p_near * (dot_nt(g, near_vals) - gdot)).astype(BF16)
        qg_ref[:, lanes(h)] = (
            dot_nn(ds_mem, mem_keys) + dot_nn(ds_near, near_keys)
        ) * scale
        rows3 = (dot_tn(ds_mem, q) * scale + dot_tn(w_mem, g)).reshape(n, rows_dev, HD)
        first_sum = jnp.sum(jnp.where(second, 0.0, rows3), axis=1, keepdims=True) * block_scale
        second_sum = jnp.sum(jnp.where(second, rows3, 0.0), axis=1, keepdims=True) * block_scale
        key_part = dot_tn(ds_near, q) * scale
        value_part = dot_tn(w_near, g)
        for d in range(n):
            here = slice(d * BLK, (d + 1) * BLK)
            pick = slot_ref[d : d + 1, :] > 0.5
            dk, dv = key_part[here], value_part[here]
            dz, dc = d // 2, d % 2
            own[h, dc, dz, 0:BLK, :] = jnp.where(pick, 0.0, dk).astype(BF16)
            own[h, dc, dz, BLK : 2 * BLK, :] = jnp.where(pick, dk, 0.0).astype(BF16)
            own[h, dc, dz, tokens : tokens + BLK, :] = (
                jnp.where(pick, 0.0, dv) + first_sum[d]
            ).astype(BF16)
            own[h, dc, dz, tokens + BLK : 2 * tokens, :] = (
                jnp.where(pick, dv, 0.0) + second_sum[d]
            ).astype(BF16)
            own[h, dc, dz, 2 * tokens :, :] = rows3[d].astype(BF16)
        sib_copy(h).start()

    def plus(a, c):
        return a.astype(F32) + c.astype(F32)

    def send_up(h, zz):
        @pl.when(z == zz)
        def _():
            for d in reversed(range(zz + 1, lines)):
                sum_up(h, d).start()

    def send_down(h, zz):
        @pl.when(z == zz)
        def _():
            for d in range(zz):
                sum_down(h, d).start()

    def sum_first(h):
        sib_copy(h).wait_recv()
        both = 2 * tokens
        acc[h, :, 0:both, :] = plus(own[h, core, :, 0:both, :], sib[h, :, 0:both, :]).astype(BF16)
        tsum[h] = plus(own[h, core, :, both:, :], sib[h, :, both:, :]).astype(BF16)
        for p in range(peers - 1):
            tsum_copy(h, p).start()

    def sum_rows(h):
        total = tsum[h, :, part(b), :].astype(F32)
        for p in range(peers - 1):
            tsum_copy(h, p).wait_recv()
            total = total + tgot[h, p].astype(F32)
        acc[h, :, 2 * tokens :, :] = total.astype(BF16)
        send_up(h, 0)
        send_down(h, last)

    def sum_next(h, k):
        @pl.when(z == k)
        def _():
            for d in reversed(range(k + 1, lines)):
                sum_up(h, d).wait_recv()
                acc[h, d] = plus(acc[h, d], ups[h, d]).astype(BF16)
                sum_up(h, d).start()

        @pl.when(z == last - k)
        def _():
            for d in range(last - k):
                sum_down(h, d).wait_recv()
                acc[h, d] = plus(acc[h, d], downs[h, d]).astype(BF16)
                sum_down(h, d).start()

    def write_sums(h, total):
        kg_ref[:, lanes(h)] = total[0:tokens]
        vg_ref[:, lanes(h)] = total[tokens : 2 * tokens]
        rows_own[h] = total[2 * tokens :].astype(BF16)

    def finish(h):
        @pl.when(z > 0)
        def _():
            sum_up(h, z).wait_recv()

        @pl.when(z < last)
        def _():
            sum_down(h, z).wait_recv()

        @pl.when(z == 0)
        def _():
            write_sums(h, plus(acc[h, 0], downs[h, 0]))

        @pl.when(z == last)
        def _():
            write_sums(h, plus(acc[h, last], ups[h, last]))

        @pl.when(jnp.logical_and(z > 0, z < last))
        def _():
            write_sums(h, plus(acc[h, z], ups[h, z]) + downs[h, z].astype(F32))

        for p in range(peers - 1):
            row_copy(h, p).start()

    def write_rows(h):
        mg_ref[part(b), lanes(h)] = rows_own[h].astype(F32)
        for p in range(peers - 1):
            row_copy(h, p).wait_recv()
            mg_ref[part((b + peers - p - 1) % peers), lanes(h)] = rows_got[h, p].astype(F32)

    stages = [(0, gather_first)]
    for k in range(1, lines):
        stages.append((k, functools.partial(gather_next, k=k)))
    stages.append((lines, compute))
    stages.append((lines + 1, sum_first))
    stages.append((lines + 2, sum_rows))
    for k in range(1, last):
        stages.append((lines + 2 + k, functools.partial(sum_next, k=k)))
    stages.append((2 * lines + 1, finish))
    stages.append((2 * lines + 2, write_rows))

    def tick(t, carry):
        for lag, stage in stages:

            @pl.when(jnp.logical_and(t >= lag, t < HEADS + lag))
            def _(lag=lag, stage=stage):
                stage(t - lag)

        return carry

    lax.fori_loop(0, HEADS + 2 * lines + 2, tick, 0)

    def drain(h, carry):
        for o in range(lines):
            kv_share(h, o).wait_send()

            @pl.when(jnp.logical_and(z < last, o <= z))
            def _(o=o):
                kv_up(h, o).wait_send()

            @pl.when(jnp.logical_and(z > 0, o >= z))
            def _(o=o):
                kv_down(h, o).wait_send()

            @pl.when(o > z)
            def _(o=o):
                sum_up(h, o).wait_send()

            @pl.when(o < z)
            def _(o=o):
                sum_down(h, o).wait_send()

        sib_copy(h).wait_send()
        for p in range(peers - 1):
            row_copy(h, p).wait_send()
            tsum_copy(h, p).wait_send()
        return carry

    lax.fori_loop(0, HEADS, drain, 0)


def fused(
    queries,
    key_states,
    value_states,
    out_grad,
    memory,
    near_device,
    near_slot,
    near_count,
    writer_block,
):
    me = lax.axis_index("seq")
    n = lax.axis_size("seq")
    peers = lax.axis_size("batch")
    lines = n // 2
    tokens = queries.shape[1]
    width = queries.shape[2]
    near_width = near_device.shape[1]
    rows_dev = MEM // n
    mine = lambda t: lax.dynamic_slice_in_dim(t, me * 2, 2, 0)
    device, slot, count = mine(near_device), mine(near_slot), mine(near_count)
    named = device[:, :, None] == jnp.arange(n)[None, None, :]
    alive = jnp.arange(near_width)[None, :] < count[:, None]
    live = jnp.any(jnp.logical_and(named, alive[:, :, None]), axis=1)
    bias = jnp.repeat(jnp.where(live, 0.0, -jnp.inf).astype(F32), BLK, axis=1)
    picked = jnp.sum(jnp.where(named, slot[:, :, None], 0), axis=(0, 1)).astype(F32)
    picked = jnp.broadcast_to(picked[:, None], (n, HD))
    quarter = rows_dev // peers
    line = 2 * tokens + quarter
    pack = 2 * tokens + rows_dev
    dma = pltpu.SemaphoreType.DMA
    vmem = pl.BlockSpec(memory_space=pltpu.VMEM)
    outs = pl.pallas_call(
        functools.partial(fused_kernel, lines, peers),
        out_shape=[jax.ShapeDtypeStruct((tokens, width), F32)] * 4
        + [jax.ShapeDtypeStruct((rows_dev, width), F32)],
        in_specs=[vmem] * 8,
        out_specs=[vmem] * 5,
        scratch_shapes=[
            pltpu.VMEM((HEADS, n, 2 * tokens, HD), BF16),
            pltpu.VMEM((HEADS, 2, lines, pack, HD), BF16),
            pltpu.VMEM((HEADS, lines, pack, HD), BF16),
            pltpu.VMEM((HEADS, lines, line, HD), BF16),
            pltpu.VMEM((HEADS, lines, line, HD), BF16),
            pltpu.VMEM((HEADS, lines, line, HD), BF16),
            pltpu.VMEM((HEADS, lines, rows_dev, HD), BF16),
            pltpu.VMEM((HEADS, peers - 1, lines, quarter, HD), BF16),
            pltpu.VMEM((n, rows_dev, HD), F32),
            pltpu.VMEM((HEADS, quarter, HD), BF16),
            pltpu.VMEM((HEADS, peers - 1, quarter, HD), BF16),
            dma((HEADS, lines)),
            dma((HEADS, lines)),
            dma((HEADS, lines)),
            dma((HEADS, n)),
            dma((HEADS,)),
            dma((HEADS,)),
            dma((HEADS, lines)),
            dma((HEADS, lines)),
            dma((HEADS, lines)),
            dma((HEADS, lines)),
            dma((HEADS, peers - 1)),
            dma((HEADS, peers - 1)),
            dma((HEADS, peers - 1)),
            dma((HEADS, peers - 1)),
        ],
        compiler_params=pltpu.CompilerParams(
            collective_id=0, has_side_effects=True, vmem_limit_bytes=60 * 1024 * 1024
        ),
    )(
        queries[0],
        key_states[0],
        value_states[0],
        out_grad[0],
        memory,
        writer_block.reshape(n, rows_dev),
        bias,
        picked,
    )
    return tuple(o.astype(BF16)[None] for o in outs[:4]) + (outs[4],)


def solution(mesh):
    placed = (P("batch", "seq", None),) * 4 + (P(),) * 5
    one_line = mesh.shape["seq"] == 8 and mesh.shape["batch"] == 4
    return jax.shard_map(
        fused if one_line else shards,
        mesh=mesh,
        in_specs=placed,
        out_specs=(P("batch", "seq", None),) * 4 + (P("seq", None),),
        check_vma=False,
    )
```

```python
import functools
import math

import jax
import jax.numpy as jnp
from jax import lax
from jax.experimental import pallas as pl
from jax.experimental.pallas import tpu as pltpu
from jax.sharding import PartitionSpec as P

HEADS = 8
HD = 128
BLK = 128
MEM = 1024
GROUPS = 2
F32 = jnp.float32
BF16 = jnp.bfloat16


def dot_nt(a, b):
    return lax.dot_general(a, b, (((1,), (1,)), ((), ())), preferred_element_type=F32)


def dot_tn(a, b):
    return lax.dot_general(a, b, (((0,), (0,)), ((), ())), preferred_element_type=F32)


def dot_nn(a, b):
    return lax.dot_general(a, b, (((1,), (0,)), ((), ())), preferred_element_type=F32)


def head_kernel(
    near_width,
    dev_ref,
    slot_ref,
    count_ref,
    q_ref,
    g_ref,
    kv_ref,
    mem_ref,
    second_ref,
    att_ref,
    qg_ref,
    out_ref,
    spread_ref,
):
    tokens = q_ref.shape[0]
    blocks = tokens // BLK
    n = kv_ref.shape[0]
    rows_dev = MEM // n
    scale = 1.0 / math.sqrt(HD)
    block_scale = 1.0 / math.sqrt(BLK)
    to_exp2 = scale * math.log2(math.e)
    values = kv_ref[:, tokens:, :].astype(F32).reshape(n, blocks, BLK, HD)
    sums = jnp.sum(values, axis=2)
    second = second_ref[...].reshape(n, rows_dev, 1) > 0.5
    add = jnp.where(second, sums[:, 1:2, :], sums[:, 0:1, :])
    mem_keys = (mem_ref[...].reshape(n, rows_dev, HD) + add * block_scale).astype(BF16)
    mem_keys = mem_keys.reshape(MEM, HD)
    term = jnp.zeros((MEM, HD), F32)
    parts = []
    for l in range(blocks):
        rows = slice(l * BLK, (l + 1) * BLK)
        q = q_ref[rows, :]
        g = g_ref[rows, :]
        keys, vals = [], []
        for j in range(near_width):
            d, s = dev_ref[l, j], slot_ref[l, j]
            keys.append(kv_ref[d, pl.ds(pl.multiple_of(s * BLK, BLK), BLK), :])
            vals.append(kv_ref[d, pl.ds(pl.multiple_of(tokens + s * BLK, BLK), BLK), :])
        near_keys = jnp.concatenate(keys, axis=0)
        near_vals = jnp.concatenate(vals, axis=0)
        s_mem = dot_nt(q, mem_keys)
        s_near = dot_nt(q, near_keys)
        live = lax.broadcasted_iota(jnp.int32, s_near.shape, 1) < count_ref[l] * BLK
        s_near = jnp.where(live, s_near, -jnp.inf)
        top = jnp.maximum(
            jnp.max(s_mem, axis=1, keepdims=True), jnp.max(s_near, axis=1, keepdims=True)
        )
        e_mem = jnp.exp2((s_mem - top) * to_exp2)
        e_near = jnp.exp2((s_near - top) * to_exp2)
        total = jnp.sum(e_mem, axis=1, keepdims=True) + jnp.sum(e_near, axis=1, keepdims=True)
        inv = 1.0 / total
        p_mem = e_mem * inv
        p_near = e_near * inv
        w_mem = p_mem.astype(BF16)
        w_near = p_near.astype(BF16)
        att = (dot_nn(w_mem, mem_keys) + dot_nn(w_near, near_vals)).astype(BF16)
        att_ref[rows, :] = att
        gdot = jnp.sum(g.astype(F32) * att.astype(F32), axis=1, keepdims=True)
        ds_mem = (p_mem * (dot_nt(g, mem_keys) - gdot)).astype(BF16)
        ds_near = (p_near * (dot_nt(g, near_vals) - gdot)).astype(BF16)
        qg_ref[rows, :] = (
            (dot_nn(ds_mem, mem_keys) + dot_nn(ds_near, near_keys)) * scale
        ).astype(BF16)
        term = term + dot_tn(ds_mem, q) * scale + dot_tn(w_mem, g)
        parts.append((dot_tn(ds_near, q) * scale, dot_tn(w_near, g)))
    rows3 = term.reshape(n, rows_dev, HD)
    first_sum = jnp.sum(jnp.where(second, 0.0, rows3), axis=1, keepdims=True) * block_scale
    second_sum = jnp.sum(jnp.where(second, rows3, 0.0), axis=1, keepdims=True) * block_scale
    spread = jnp.concatenate([first_sum, second_sum], axis=1)
    spread_ref[...] = spread
    out_ref[:, 0:tokens, :] = jnp.zeros((n, tokens, HD), BF16)
    for s in range(blocks):
        out_ref[:, tokens + s * BLK : tokens + (s + 1) * BLK, :] = jnp.broadcast_to(
            spread[:, s : s + 1, :], (n, BLK, HD)
        ).astype(BF16)
    out_ref[:, 2 * tokens :, :] = rows3.astype(BF16)
    for l in range(blocks):
        for j in range(near_width):
            d, s = dev_ref[l, j], slot_ref[l, j]
            here = slice(j * BLK, (j + 1) * BLK)
            row = spread_ref[d, pl.ds(s, 1), :]
            out_ref[d, pl.ds(pl.multiple_of(s * BLK, BLK), BLK), :] = parts[l][0][here].astype(BF16)
            out_ref[d, pl.ds(pl.multiple_of(tokens + s * BLK, BLK), BLK), :] = (
                parts[l][1][here] + row
            ).astype(BF16)


def attend_group(group, heads, tables, queries, out_grad, kv, memory, second):
    tokens = queries.shape[0]
    n = kv.shape[0]
    near_width = tables[0].shape[1]
    rows_dev = MEM // n
    first = group * heads
    width = heads * HD
    whole = lambda h, *_: (0, first + h)
    part = lambda h, *_: (0, h)
    part3 = lambda h, *_: (0, 0, h)
    keys = MEM + near_width * BLK
    return pl.pallas_call(
        functools.partial(head_kernel, near_width),
        out_shape=(
            jax.ShapeDtypeStruct((tokens, width), BF16),
            jax.ShapeDtypeStruct((tokens, width), BF16),
            jax.ShapeDtypeStruct((n, 2 * tokens + rows_dev, width), BF16),
        ),
        grid_spec=pltpu.PrefetchScalarGridSpec(
            num_scalar_prefetch=3,
            grid=(heads,),
            in_specs=[
                pl.BlockSpec((tokens, HD), whole),
                pl.BlockSpec((tokens, HD), whole),
                pl.BlockSpec((n, 2 * tokens, HD), part3),
                pl.BlockSpec((MEM, HD), whole),
                pl.BlockSpec((MEM, 1), lambda h, *_: (0, 0)),
            ],
            out_specs=(
                pl.BlockSpec((tokens, HD), part),
                pl.BlockSpec((tokens, HD), part),
                pl.BlockSpec((n, 2 * tokens + rows_dev, HD), part3),
            ),
            scratch_shapes=[pltpu.VMEM((n, tokens // BLK, HD), F32)],
        ),
        compiler_params=pltpu.CompilerParams(
            dimension_semantics=("arbitrary",), vmem_limit_bytes=50 * 1024 * 1024
        ),
        cost_estimate=pl.CostEstimate(
            flops=12 * tokens * keys * width,
            bytes_accessed=n * tokens * width * 10,
            transcendentals=heads * tokens * keys,
        ),
    )(*tables, queries, out_grad, kv, memory, second)


def shards(
    queries,
    key_states,
    value_states,
    out_grad,
    memory,
    near_device,
    near_slot,
    near_count,
    writer_block,
):
    my_index = lax.axis_index("seq")
    tokens = queries.shape[1]
    local_blocks = tokens // BLK
    heads = HEADS // GROUPS
    width = heads * HD
    mine = lambda t: lax.dynamic_slice_in_dim(t, my_index * local_blocks, local_blocks, 0)
    tables = (mine(near_device), mine(near_slot), mine(near_count))
    second = (writer_block % local_blocks).astype(F32).reshape(MEM, 1)
    gathered = []
    for group in range(GROUPS):
        cols = slice(group * width, (group + 1) * width)
        packed = jnp.concatenate([key_states[0][:, cols], value_states[0][:, cols]], axis=0)
        gathered.append(lax.all_gather(packed, "seq", axis=0, tiled=False))
    results = []
    for group in range(GROUPS):
        att, qg, out = attend_group(
            group, heads, tables, queries[0], out_grad[0], gathered[group], memory, second
        )
        got = lax.psum_scatter(out, "seq", scatter_dimension=0, tiled=False)
        results.append((att, qg, got[:tokens], got[tokens : 2 * tokens], got[2 * tokens :]))
    att, qg, kg, vg, rows = [jnp.concatenate(c, axis=1) for c in zip(*results)]
    memory_grad = lax.psum(rows, "batch").astype(F32)
    return (att[None], qg[None], kg[None], vg[None], memory_grad)


MESH = pl.DeviceIdType.MESH


def fused_kernel(
    lines,
    peers,
    q_ref,
    k_ref,
    v_ref,
    g_ref,
    mem_ref,
    writer_ref,
    bias_ref,
    slot_ref,
    att_ref,
    qg_ref,
    kg_ref,
    vg_ref,
    mg_ref,
    kv,
    own,
    sib,
    ups,
    downs,
    acc,
    tsum,
    tgot,
    second_mask,
    rows_own,
    rows_got,
    up_send,
    down_send,
    share_send,
    kv_recv,
    sib_send,
    sib_recv,
    ups_send,
    ups_recv,
    downs_send,
    downs_recv,
    tsum_send,
    tsum_recv,
    rows_send,
    rows_recv,
):
    n = 2 * lines
    tokens = q_ref.shape[0]
    rows_dev = MEM // n
    scale = 1.0 / math.sqrt(HD)
    block_scale = 1.0 / math.sqrt(BLK)
    to_exp2 = scale * math.log2(math.e)
    me = lax.axis_index("seq")
    b = lax.axis_index("batch")
    z, core = me // 2, me % 2
    last = lines - 1
    quarter = rows_dev // peers

    def at(zz, cc):
        return (b, zz * 2 + cc)

    barrier = pltpu.get_barrier_semaphore()

    @pl.when(z < last)
    def _():
        pl.semaphore_signal(barrier, inc=1, device_id=at(z + 1, core), device_id_type=MESH)

    @pl.when(z > 0)
    def _():
        pl.semaphore_signal(barrier, inc=1, device_id=at(z - 1, core), device_id_type=MESH)

    pl.semaphore_signal(barrier, inc=1, device_id=at(z, 1 - core), device_id_type=MESH)
    for p in range(1, peers):
        pl.semaphore_signal(barrier, inc=1, device_id=((b + p) % peers, me), device_id_type=MESH)
    edges = jnp.where(z < last, 1, 0) + jnp.where(z > 0, 1, 0)
    pl.semaphore_wait(barrier, edges + peers)

    def send(src, dst, s, r, dev):
        return pltpu.make_async_remote_copy(
            src_ref=src, dst_ref=dst, send_sem=s, recv_sem=r, device_id=dev, device_id_type=MESH
        )

    def kv_up(h, o):
        i = o * 2 + core
        return send(
            kv.at[h, i], kv.at[h, i], up_send.at[h, o], kv_recv.at[h, i], at((z + 1) % lines, core)
        )

    def kv_down(h, o):
        i = o * 2 + core
        return send(
            kv.at[h, i],
            kv.at[h, i],
            down_send.at[h, o],
            kv_recv.at[h, i],
            at((z + last) % lines, core),
        )

    def kv_share(h, o):
        i = o * 2 + core
        return send(
            kv.at[h, i], kv.at[h, i], share_send.at[h, o], kv_recv.at[h, i], at(z, 1 - core)
        )

    def kv_got(h, o, c):
        i = o * 2 + c
        send(
            kv.at[h, i], kv.at[h, i], share_send.at[h, o], kv_recv.at[h, i], at(z, 1 - core)
        ).wait_recv()

    def sib_copy(h):
        return send(own.at[h, 1 - core], sib.at[h], sib_send.at[h], sib_recv.at[h], at(z, 1 - core))

    def sum_up(h, d):
        return send(
            acc.at[h, d],
            ups.at[h, d],
            ups_send.at[h, d],
            ups_recv.at[h, d],
            at((z + 1) % lines, core),
        )

    def sum_down(h, d):
        return send(
            acc.at[h, d],
            downs.at[h, d],
            downs_send.at[h, d],
            downs_recv.at[h, d],
            at((z + last) % lines, core),
        )

    def row_copy(h, p):
        return send(
            rows_own.at[h],
            rows_got.at[h, p],
            rows_send.at[h, p],
            rows_recv.at[h, p],
            ((b + p + 1) % peers, me),
        )

    def part(p):
        return pl.ds(pl.multiple_of(p * quarter, quarter), quarter)

    def tsum_copy(h, p):
        peer = (b + p + 1) % peers
        return send(
            tsum.at[h, :, part(peer), :],
            tgot.at[h, p],
            tsum_send.at[h, p],
            tsum_recv.at[h, p],
            (peer, me),
        )

    for d in range(n):
        odd = (writer_ref[d : d + 1, :] % 2).astype(F32)
        second_mask[d] = jnp.broadcast_to(odd, (rows_dev, HD)).T

    def lanes(h):
        return pl.ds(pl.multiple_of(h * HD, HD), HD)

    def gather_ends(t):
        for h in (2 * t, 2 * t + 1):
            kv[h, me, 0:tokens, :] = k_ref[:, lanes(h)]
            kv[h, me, tokens : 2 * tokens, :] = v_ref[:, lanes(h)]

            @pl.when(z == 0)
            def _(h=h):
                kv_up(h, 0).start()

            @pl.when(z == last)
            def _(h=h):
                kv_down(h, last).start()

    def gather_first(h):
        @pl.when(jnp.logical_and(z > 0, z < last))
        def _():
            kv_up(h, z).start()
            kv_down(h, z).start()

        kv_share(h, z).start()

    def gather_next(h, k):
        @pl.when(z >= k)
        def _():
            kv_got(h, z - k, core)

            @pl.when(z < last)
            def _():
                kv_up(h, z - k).start()

            kv_share(h, z - k).start()

        @pl.when(z + k <= last)
        def _():
            kv_got(h, z + k, core)

            @pl.when(z > 0)
            def _():
                kv_down(h, z + k).start()

            kv_share(h, z + k).start()

    def compute(h):
        for o in range(lines):
            kv_got(h, o, 1 - core)
        q = q_ref[:, lanes(h)]
        g = g_ref[:, lanes(h)]
        values = kv[h, :, tokens:, :].astype(F32).reshape(n, 2, BLK, HD)
        sums = jnp.sum(values, axis=2)
        second = second_mask[...] > 0.5
        add = jnp.where(second, sums[:, 1:2, :], sums[:, 0:1, :])
        mem_keys = (mem_ref[:, lanes(h)].reshape(n, rows_dev, HD) + add * block_scale).astype(BF16)
        mem_keys = mem_keys.reshape(MEM, HD)
        keys, vals = [], []
        for d in range(n):
            pick = slot_ref[d : d + 1, :] > 0.5
            pair = lambda start: jnp.where(
                pick,
                kv[h, d, start + BLK : start + 2 * BLK, :].astype(F32),
                kv[h, d, start : start + BLK, :].astype(F32),
            ).astype(BF16)
            keys.append(pair(0))
            vals.append(pair(tokens))
        near_keys = jnp.concatenate(keys, axis=0)
        near_vals = jnp.concatenate(vals, axis=0)
        bias = jnp.concatenate(
            [jnp.broadcast_to(bias_ref[l : l + 1, :], (BLK, n * BLK)) for l in range(2)], axis=0
        )
        s_mem = dot_nt(q, mem_keys)
        s_near = dot_nt(q, near_keys) + bias
        top = jnp.maximum(
            jnp.max(s_mem, axis=1, keepdims=True), jnp.max(s_near, axis=1, keepdims=True)
        )
        e_mem = jnp.exp2((s_mem - top) * to_exp2)
        e_near = jnp.exp2((s_near - top) * to_exp2)
        inv = 1.0 / (
            jnp.sum(e_mem, axis=1, keepdims=True) + jnp.sum(e_near, axis=1, keepdims=True)
        )
        p_mem = e_mem * inv
        p_near = e_near * inv
        w_mem = p_mem.astype(BF16)
        w_near = p_near.astype(BF16)
        att = (dot_nn(w_mem, mem_keys) + dot_nn(w_near, near_vals)).astype(BF16)
        att = att.astype(F32)
        att_ref[:, lanes(h)] = att
        gdot = jnp.sum(g.astype(F32) * att, axis=1, keepdims=True)
        ds_mem = (p_mem * (dot_nt(g, mem_keys) - gdot)).astype(BF16)
        ds_near = (p_near * (dot_nt(g, near_vals) - gdot)).astype(BF16)
        qg_ref[:, lanes(h)] = (
            dot_nn(ds_mem, mem_keys) + dot_nn(ds_near, near_keys)
        ) * scale
        rows3 = (dot_tn(ds_mem, q) * scale + dot_tn(w_mem, g)).reshape(n, rows_dev, HD)
        first_sum = jnp.sum(jnp.where(second, 0.0, rows3), axis=1, keepdims=True) * block_scale
        second_sum = jnp.sum(jnp.where(second, rows3, 0.0), axis=1, keepdims=True) * block_scale
        key_part = dot_tn(ds_near, q) * scale
        value_part = dot_tn(w_near, g)
        for d in range(n):
            here = slice(d * BLK, (d + 1) * BLK)
            pick = slot_ref[d : d + 1, :] > 0.5
            dk, dv = key_part[here], value_part[here]
            dz, dc = d // 2, d % 2
            own[h, dc, dz, 0:BLK, :] = jnp.where(pick, 0.0, dk).astype(BF16)
            own[h, dc, dz, BLK : 2 * BLK, :] = jnp.where(pick, dk, 0.0).astype(BF16)
            own[h, dc, dz, tokens : tokens + BLK, :] = (
                jnp.where(pick, 0.0, dv) + first_sum[d]
            ).astype(BF16)
            own[h, dc, dz, tokens + BLK : 2 * tokens, :] = (
                jnp.where(pick, dv, 0.0) + second_sum[d]
            ).astype(BF16)
            own[h, dc, dz, 2 * tokens :, :] = rows3[d].astype(BF16)
        sib_copy(h).start()

    def plus(a, c):
        return a.astype(F32) + c.astype(F32)

    def send_up(h, zz):
        @pl.when(z == zz)
        def _():
            for d in reversed(range(zz + 1, lines)):
                sum_up(h, d).start()

    def send_down(h, zz):
        @pl.when(z == zz)
        def _():
            for d in range(zz):
                sum_down(h, d).start()

    def sum_first(h):
        sib_copy(h).wait_recv()
        both = 2 * tokens
        acc[h, :, 0:both, :] = plus(own[h, core, :, 0:both, :], sib[h, :, 0:both, :]).astype(BF16)
        tsum[h] = plus(own[h, core, :, both:, :], sib[h, :, both:, :]).astype(BF16)
        for p in range(peers - 1):
            tsum_copy(h, p).start()

    def sum_rows(h):
        total = tsum[h, :, part(b), :].astype(F32)
        for p in range(peers - 1):
            tsum_copy(h, p).wait_recv()
            total = total + tgot[h, p].astype(F32)
        acc[h, :, 2 * tokens :, :] = total.astype(BF16)
        send_up(h, 0)
        send_down(h, last)

    def sum_next(h, k):
        @pl.when(z == k)
        def _():
            for d in reversed(range(k + 1, lines)):
                sum_up(h, d).wait_recv()
                acc[h, d] = plus(acc[h, d], ups[h, d]).astype(BF16)
                sum_up(h, d).start()

        @pl.when(z == last - k)
        def _():
            for d in range(last - k):
                sum_down(h, d).wait_recv()
                acc[h, d] = plus(acc[h, d], downs[h, d]).astype(BF16)
                sum_down(h, d).start()

    def write_sums(h, total):
        kg_ref[:, lanes(h)] = total[0:tokens]
        vg_ref[:, lanes(h)] = total[tokens : 2 * tokens]
        rows_own[h] = total[2 * tokens :].astype(BF16)

    def finish(h):
        @pl.when(z > 0)
        def _():
            sum_up(h, z).wait_recv()

        @pl.when(z < last)
        def _():
            sum_down(h, z).wait_recv()

        @pl.when(z == 0)
        def _():
            write_sums(h, plus(acc[h, 0], downs[h, 0]))

        @pl.when(z == last)
        def _():
            write_sums(h, plus(acc[h, last], ups[h, last]))

        @pl.when(jnp.logical_and(z > 0, z < last))
        def _():
            write_sums(h, plus(acc[h, z], ups[h, z]) + downs[h, z].astype(F32))

        for p in range(peers - 1):
            row_copy(h, p).start()

    def write_rows(h):
        mg_ref[part(b), lanes(h)] = rows_own[h].astype(F32)
        for p in range(peers - 1):
            row_copy(h, p).wait_recv()
            mg_ref[part((b + peers - p - 1) % peers), lanes(h)] = rows_got[h, p].astype(F32)

    stages = [(0, gather_first)]
    for k in range(1, lines):
        stages.append((k, functools.partial(gather_next, k=k)))
    stages.append((lines, compute))
    stages.append((lines + 1, sum_first))
    stages.append((lines + 2, sum_rows))
    for k in range(1, last):
        stages.append((lines + 2 + k, functools.partial(sum_next, k=k)))
    stages.append((2 * lines + 1, finish))
    stages.append((2 * lines + 2, write_rows))

    def tick(t, carry):
        @pl.when(t < HEADS // 2)
        def _():
            gather_ends(t)

        for lag, stage in stages:

            @pl.when(jnp.logical_and(t >= lag, t < HEADS + lag))
            def _(lag=lag, stage=stage):
                stage(t - lag)

        return carry

    lax.fori_loop(0, HEADS + 2 * lines + 2, tick, 0)

    def drain(h, carry):
        for o in range(lines):
            kv_share(h, o).wait_send()

            @pl.when(jnp.logical_and(z < last, o <= z))
            def _(o=o):
                kv_up(h, o).wait_send()

            @pl.when(jnp.logical_and(z > 0, o >= z))
            def _(o=o):
                kv_down(h, o).wait_send()

            @pl.when(o > z)
            def _(o=o):
                sum_up(h, o).wait_send()

            @pl.when(o < z)
            def _(o=o):
                sum_down(h, o).wait_send()

        sib_copy(h).wait_send()
        for p in range(peers - 1):
            row_copy(h, p).wait_send()
            tsum_copy(h, p).wait_send()
        return carry

    lax.fori_loop(0, HEADS, drain, 0)


def fused(
    queries,
    key_states,
    value_states,
    out_grad,
    memory,
    near_device,
    near_slot,
    near_count,
    writer_block,
):
    me = lax.axis_index("seq")
    n = lax.axis_size("seq")
    peers = lax.axis_size("batch")
    lines = n // 2
    tokens = queries.shape[1]
    width = queries.shape[2]
    near_width = near_device.shape[1]
    rows_dev = MEM // n
    mine = lambda t: lax.dynamic_slice_in_dim(t, me * 2, 2, 0)
    device, slot, count = mine(near_device), mine(near_slot), mine(near_count)
    named = device[:, :, None] == jnp.arange(n)[None, None, :]
    alive = jnp.arange(near_width)[None, :] < count[:, None]
    live = jnp.any(jnp.logical_and(named, alive[:, :, None]), axis=1)
    bias = jnp.repeat(jnp.where(live, 0.0, -jnp.inf).astype(F32), BLK, axis=1)
    picked = jnp.sum(jnp.where(named, slot[:, :, None], 0), axis=(0, 1)).astype(F32)
    picked = jnp.broadcast_to(picked[:, None], (n, HD))
    quarter = rows_dev // peers
    line = 2 * tokens + quarter
    pack = 2 * tokens + rows_dev
    dma = pltpu.SemaphoreType.DMA
    vmem = pl.BlockSpec(memory_space=pltpu.VMEM)
    outs = pl.pallas_call(
        functools.partial(fused_kernel, lines, peers),
        out_shape=[jax.ShapeDtypeStruct((tokens, width), F32)] * 4
        + [jax.ShapeDtypeStruct((rows_dev, width), F32)],
        in_specs=[vmem] * 8,
        out_specs=[vmem] * 5,
        scratch_shapes=[
            pltpu.VMEM((HEADS, n, 2 * tokens, HD), BF16),
            pltpu.VMEM((HEADS, 2, lines, pack, HD), BF16),
            pltpu.VMEM((HEADS, lines, pack, HD), BF16),
            pltpu.VMEM((HEADS, lines, line, HD), BF16),
            pltpu.VMEM((HEADS, lines, line, HD), BF16),
            pltpu.VMEM((HEADS, lines, line, HD), BF16),
            pltpu.VMEM((HEADS, lines, rows_dev, HD), BF16),
            pltpu.VMEM((HEADS, peers - 1, lines, quarter, HD), BF16),
            pltpu.VMEM((n, rows_dev, HD), F32),
            pltpu.VMEM((HEADS, quarter, HD), BF16),
            pltpu.VMEM((HEADS, peers - 1, quarter, HD), BF16),
            dma((HEADS, lines)),
            dma((HEADS, lines)),
            dma((HEADS, lines)),
            dma((HEADS, n)),
            dma((HEADS,)),
            dma((HEADS,)),
            dma((HEADS, lines)),
            dma((HEADS, lines)),
            dma((HEADS, lines)),
            dma((HEADS, lines)),
            dma((HEADS, peers - 1)),
            dma((HEADS, peers - 1)),
            dma((HEADS, peers - 1)),
            dma((HEADS, peers - 1)),
        ],
        compiler_params=pltpu.CompilerParams(
            collective_id=0, has_side_effects=True, vmem_limit_bytes=60 * 1024 * 1024
        ),
    )(
        queries[0],
        key_states[0],
        value_states[0],
        out_grad[0],
        memory,
        writer_block.reshape(n, rows_dev),
        bias,
        picked,
    )
    return tuple(o.astype(BF16)[None] for o in outs[:4]) + (outs[4],)


def solution(mesh):
    placed = (P("batch", "seq", None),) * 4 + (P(),) * 5
    one_line = mesh.shape["seq"] == 8 and mesh.shape["batch"] == 4
    return jax.shard_map(
        fused if one_line else shards,
        mesh=mesh,
        in_specs=placed,
        out_specs=(P("batch", "seq", None),) * 4 + (P("seq", None),),
        check_vma=False,
    )
```
